32 devices in a mesh: chan: 8 (over z, y), win: 4 (over x, core).
Axes of the slice: x: 2, y: 2, z: 4, core: 2. Of those that a mesh axis runs over, the one named last changes fastest.
Arguments:
- traces: float32 [64, 49152], P('chan', 'win')
- offsets: int32 [4], P('win'), may hold values from 0 to 4096
- pair_source: int32 [8, 24], P('chan'), may hold values from 0 to 7
- pair_recv: int32 [8, 24], P('chan'), may hold values from 0 to 7
- pair_hop: int32 [8, 24], P('chan'), may hold values from 0 to 6, never falling along the last dimension, each value on 1 to 6 neighbouring positions
- pair_owner: int32 [192, 1], P('chan'), may hold values from 0 to 7; in each aligned block of 24 rows (0 to 23, 24 to 47, ...) at most 6 rows name the same one
Outputs:
- stacks: float32 [384, 2, 2048], P('chan', None, 'win')
The draws below stay inside these ranges and needn't reach their ends.
Inputs may be any that keep to these rules, and one draw needn't show every extreme that they name: `pair_hop`: within each block the pairs are ordered by offset index; every offset index has 1 to 6 pairs in a block, and some has exactly 6. `pair_owner`: at most 6 pairs of one block feed one owner, and some owner gets exactly 6.
All inputs are finite; a program needn't handle non-finite values.
Results may differ from the reference program's by a relative error of at most 0.022.
Values may be sent and summed in bfloat16 or wider, within the bound.
No kernel may reach another device: no remote copies, remote signals or barrier semaphores. Data moves between devices by JAX's collectives and lax.ppermute only.
A program may use at most 128 MiB of HBM per device.

```python
import math
import jax
import jax.numpy as jnp
import numpy as np
from jax import lax

NT = 8192
F = 2048
SMOOTH_HALF = 32
CH_DEV = 8
SEG_DEV = 1
PAIRS_BLK = 24
HOPS = 3
OFFS = 7
HMOST = 6
CAP = 6
FX = 2112
REC = 12288
CHANNELS = 64
RECORD = 49152
WINDOWS = 4
PAIRS = 192
STACK_ROWS = 384
N_CHAN = 8
N_WIN = 4


def draw_traces(key, part):
    keys = jax.random.split(key, 3)
    blocking = NT // 8
    pieces = RECORD // blocking
    channel_gain = jnp.exp(jax.random.uniform(keys[1], (CHANNELS, 1, 1), jnp.float32, 0.0, math.log(10.0)))
    block_gain = jnp.exp(jax.random.uniform(keys[2], (CHANNELS, pieces, 1), jnp.float32, 0.0, math.log(10.0)))
    noise = jax.random.normal(keys[0], (CHANNELS, pieces, blocking), jnp.float32)
    return (noise * channel_gain * block_gain).reshape(CHANNELS, RECORD)


def plant(values, own_key, smallest, high):
    dims = values.shape
    spot = [jax.random.randint(jax.random.fold_in(own_key, axis), (), 0, dims[axis]) for axis in range(len(dims))]
    values = values.at[tuple(spot)].set(smallest)
    longest = dims.index(max(dims))
    spot[longest] = (spot[longest] + 1) % dims[longest]
    return values.at[tuple(spot)].set(high)


def length_profile(amount, total, limit, slope):
    portions = [(1 << 20) // math.isqrt(grade ** slope) + 1 for grade in range(2, amount + 1)]
    rest, counts = total - limit - (amount - 1), [1] * (amount - 1)
    while rest > 0:
        movable = [i for i in range(amount - 1) if counts[i] < limit]
        whole, budget = sum([portions[i] for i in movable]), rest
        for i in movable:
            more = min(limit - counts[i], max(1, budget * portions[i] // whole), rest)
            counts[i] = counts[i] + more
            rest = rest - more
    return np.array([limit] + counts)


def ragged_sizes(own_key, number_of, total, bound, slope):
    if number_of == 2:
        one = jax.random.randint(own_key, (), max(1, total - bound), min(bound, total - 1) + 1)
        return jnp.stack([one, total - one])
    tallies = jnp.asarray(length_profile(number_of, total, bound, slope), jnp.int32)
    couples = (number_of - 1) // 2
    donor, taker = tallies[1:1 + 2 * couples:2], tallies[2:2 + 2 * couples:2]
    room = jnp.minimum(donor - 1, bound - taker)
    passed = jax.random.randint(jax.random.fold_in(own_key, 1), (couples,), 0, 1 << 20) % (room + 1)
    tallies = tallies.at[1:1 + 2 * couples:2].set(donor - passed).at[2:2 + 2 * couples:2].set(taker + passed)
    return tallies[jax.random.permutation(jax.random.fold_in(own_key, 2), number_of)]


def routed_block(rng, own, number, rows, number_of, top, limit, lean):
    sequence = jax.random.permutation(rng, number_of)
    heavy_load, usual = shares(number_of, rows * top, limit, lean, True), shares(number_of, rows * top, limit, lean, False)
    places = jnp.arange(number_of)

    def named(tallies, rotation):
        used = int((tallies > 0).sum())
        fixed = max(1, used // 4)
        shifted = fixed + (places - fixed + rotation * (used - fixed)) % max(1, number_of - fixed)
        return jnp.zeros((number_of,), jnp.int32).at[sequence[jnp.where(places < fixed, places, shifted)]].set(jnp.asarray(tallies, jnp.int32))

    tallies = jnp.where(number % 4 == 0, named(heavy_load, number // 4), named(usual, number - number // 4 - 1))
    mixed = jax.random.permutation(jax.random.fold_in(own, 3), number_of)
    giver, receiver = mixed[0:number_of // 2 * 2:2], mixed[1:number_of // 2 * 2:2]
    room = jnp.minimum(tallies[giver] - 1, limit - tallies[receiver]) // 2
    room = jnp.where((giver == sequence[0]) | (receiver == sequence[0]) | (tallies[receiver] == 0), 0, jnp.maximum(room, 0))
    shifted = jax.random.randint(jax.random.fold_in(own, 4), (number_of // 2,), 0, 1 << 20) % (room + 1)
    tallies = tallies.at[giver].add(-shifted).at[receiver].add(shifted)
    labels = jnp.searchsorted(jnp.cumsum(tallies), jnp.arange(rows * top), side="right").astype(jnp.int32)
    table = labels.reshape(top, rows).T
    table = table[jax.random.permutation(jax.random.fold_in(own, 1), rows)]
    rotation = jax.random.randint(jax.random.fold_in(own, 2), (rows, 1), 0, top)
    return jnp.take_along_axis(table, (jnp.arange(top)[None, :] + rotation) % top, axis=1)


def shares(amount, total, bound, lean, full):
    loads = [(1 << 20) // math.isqrt(grade ** lean) + 1 for grade in range(1, amount + 1)]
    largest = bound if full else min(bound, max(-(-total // amount), total * loads[0] // sum(loads)))
    least = 1 if total - largest >= amount - 1 else 0
    given, surplus = [largest] + [least] * (amount - 1), total - largest - least * (amount - 1)
    while surplus > 0:
        candidates = [i for i in range(1, amount) if given[i] < largest] or [i for i in range(1, amount) if given[i] < bound]
        mass, budget = sum([loads[i] for i in candidates]), surplus
        for i in candidates:
            more = min(bound - given[i], max(1, budget * loads[i] // mass), surplus)
            given[i] = given[i] + more
            surplus = surplus - more
    return np.array(given)


def setup_inputs(seed: int = 0) -> dict:
    arg_keys = jax.random.split(jax.random.key(seed), 7)
    traces = draw_traces(jax.random.fold_in(arg_keys[6], 71), 0)
    offsets = plant(jax.random.randint(arg_keys[1], (WINDOWS,), 0, REC - NT + 1), jax.random.fold_in(arg_keys[1], 1), 0, REC - NT).astype(jnp.int32)
    pair_source = plant(jax.random.randint(arg_keys[2], (N_CHAN, PAIRS_BLK), 0, CH_DEV), jax.random.fold_in(arg_keys[2], 1), 0, CH_DEV - 1).astype(jnp.int32)
    pair_recv = plant(jax.random.randint(arg_keys[3], (N_CHAN, PAIRS_BLK), 0, CH_DEV), jax.random.fold_in(arg_keys[3], 1), 0, CH_DEV - 1).astype(jnp.int32)
    pair_hop = jax.vmap(lambda own: jnp.searchsorted(jnp.cumsum(ragged_sizes(own, OFFS, PAIRS_BLK, HMOST, 2)), jnp.arange(PAIRS_BLK), side="right"))(jax.random.split(arg_keys[4], N_CHAN)).reshape((N_CHAN, PAIRS_BLK)).astype(jnp.int32)
    pair_owner_keys = jax.random.split(jax.random.fold_in(arg_keys[5], 1), PAIRS // PAIRS_BLK)
    pair_owner_turns = jax.random.permutation(jax.random.fold_in(arg_keys[5], 3), PAIRS // PAIRS_BLK)
    pair_owner = jax.vmap(lambda own, number: routed_block(jax.random.fold_in(arg_keys[5], 2), own, number, PAIRS_BLK, N_CHAN, 1, CAP, 2))(pair_owner_keys, pair_owner_turns).reshape((PAIRS, 1))
    return dict(traces=traces, offsets=offsets, pair_source=pair_source, pair_recv=pair_recv, pair_hop=pair_hop, pair_owner=pair_owner)


def whiten_rows(segment):
    centred = segment - lax.optimization_barrier(jnp.mean(segment, axis=1, keepdims=True))
    positions = jnp.arange(NT, dtype=jnp.int32).astype(segment.dtype)
    taper = 0.5 - 0.5 * jnp.cos(2.0 * math.pi / NT * positions)
    spectrum = jnp.fft.rfft(centred * taper, axis=1)[:, :FX]
    real_part = jnp.real(spectrum).astype(segment.dtype)
    imag_part = jnp.imag(spectrum).astype(segment.dtype)
    power = real_part * real_part + imag_part * imag_part
    level = lax.reduce_window(power, jnp.zeros((), power.dtype), lax.add, (1, 2 * SMOOTH_HALF + 1), (1, 1), 'VALID') / (2 * SMOOTH_HALF + 1)
    scale = lax.rsqrt(level + 1e-06)
    kept_real = real_part[:, SMOOTH_HALF:SMOOTH_HALF + F] * scale
    kept_imag = imag_part[:, SMOOTH_HALF:SMOOTH_HALF + F] * scale
    return jnp.stack([kept_real, kept_imag], axis=1).astype(jnp.bfloat16)

def reference(traces, offsets, pair_source, pair_recv, pair_hop, pair_owner):

    def one_window(index):
        start = (index // SEG_DEV * REC + offsets[index]).astype(jnp.int32)
        segment = lax.dynamic_slice_in_dim(traces, start, NT, 1)
        return whiten_rows(segment)
    white = lax.map(one_window, jnp.arange(WINDOWS, dtype=jnp.int32))
    owners_all = pair_owner.reshape(N_CHAN, PAIRS_BLK)

    def one_block(block):
        source_ids = block * CH_DEV + pair_source[block]
        target_block = (block + pair_hop[block] - HOPS) % N_CHAN
        receiver_ids = target_block * CH_DEV + pair_recv[block]
        sources = jnp.take(white, source_ids, axis=1).astype(jnp.float32)
        receivers = jnp.take(white, receiver_ids, axis=1).astype(jnp.float32)
        real_part = sources[:, :, 0] * receivers[:, :, 0] + sources[:, :, 1] * receivers[:, :, 1]
        imag_part = sources[:, :, 0] * receivers[:, :, 1] - sources[:, :, 1] * receivers[:, :, 0]
        terms = jnp.stack([real_part, imag_part], axis=2)
        partial_value = lax.optimization_barrier(jnp.sum(terms.reshape(N_WIN, SEG_DEV, PAIRS_BLK, 2, F), axis=1))
        rounded = lax.optimization_barrier(partial_value.astype(jnp.bfloat16)).astype(jnp.float32)
        cross = lax.optimization_barrier(jnp.sum(rounded, axis=0))
        owners = owners_all[block]
        onehot = (owners[:, None] == jnp.arange(N_CHAN, dtype=jnp.int32)[None, :]).astype(jnp.int32)
        earlier = jnp.cumsum(onehot, axis=0) - onehot
        slot = lax.optimization_barrier(jnp.sum(earlier * onehot, axis=1))
        rows = owners * (N_CHAN * CAP) + block * CAP + slot
        return (cross, rows.astype(jnp.int32))
    crosses, rows = lax.map(one_block, jnp.arange(N_CHAN, dtype=jnp.int32))
    stacks = jnp.zeros((STACK_ROWS, 2, F), jnp.float32)
    return stacks.at[rows.reshape(-1)].set(crosses.reshape(-1, 2, F).astype(jnp.float32))
```

```python
import functools
import math

import jax
import jax.numpy as jnp
import numpy as np
from jax import lax
from jax.experimental import pallas as pl
from jax.experimental.pallas import tpu as pltpu
from jax.sharding import PartitionSpec as P

NT = 8192
F = 2048
SMOOTH_HALF = 32
LANES = 128
HIGH = NT // LANES
ROWS = F // LANES
GRID_ROWS = 24
F32 = jnp.float32
BF16 = jnp.bfloat16
HIGHEST = lax.Precision.HIGHEST


def tables():
    lane = np.arange(LANES)
    high = np.arange(HIGH)
    first = 2 * np.pi / HIGH * (np.outer(np.arange(HIGH) + SMOOTH_HALF, high) % HIGH)
    first = np.concatenate([np.cos(first), -np.sin(first)], axis=0)
    twist = 2 * np.pi / NT * (np.outer(lane + SMOOTH_HALF, lane) % NT)
    twist = np.stack([np.cos(twist), -np.sin(twist)])
    grid_row = np.arange(GRID_ROWS) - 1
    second = 2 * np.pi / HIGH * (np.outer(grid_row, lane) % HIGH)
    cos, sin = np.cos(second), -np.sin(second)
    live = (np.arange(GRID_ROWS) < ROWS + 2)[:, None]
    cos, sin = cos * live, sin * live
    second = np.concatenate(
        [np.concatenate([cos, -sin], axis=1), np.concatenate([sin, cos], axis=1)], axis=0
    )
    phase = 2 * np.pi / NT * np.arange(NT).reshape(HIGH, LANES)
    wave = np.stack([np.cos(phase), np.sin(phase)])
    source = np.arange(3 * LANES)[:, None] - LANES
    band = np.abs(source - lane[None, :]) <= SMOOTH_HALF
    return (
        first.astype(np.float32),
        twist.astype(np.float32),
        second.astype(np.float32),
        wave.astype(np.float32),
        band.astype(jnp.bfloat16),
    )


def split(value):
    top = value.astype(BF16)
    return top, (value - top.astype(F32)).astype(BF16)


def whiten_kernel(
    scalars, traces, source, receiver, hop, owner, first, twist, second, wave, band, *rest
):
    outs, (centred, grid_real, grid_imag, white) = rest[:-4], rest[-4:]
    windows = len(outs) - 1
    channels = traces.shape[0]
    offset, me = scalars[0], scalars[1]

    lane = lax.broadcasted_iota(jnp.int32, (channels, LANES), 1)
    total = jnp.zeros((channels, LANES), F32)
    blocks = []
    spare = traces.shape[1] // LANES - HIGH
    for i in range(HIGH):
        piece = traces[:, i * LANES : (i + 1) * LANES]
        if i < spare:
            later = traces[:, (i + HIGH) * LANES : (i + HIGH + 1) * LANES]
            piece = jnp.where(lane + i * LANES >= offset, piece, later)
        centred[i * channels : (i + 1) * channels, :] = piece
        total = total + piece
    mean = jnp.sum(total, axis=1, keepdims=True) * (1.0 / NT)
    centred[...] = centred[...] - jnp.tile(mean, (HIGH, 1))

    angle = jnp.full((8, LANES), offset, jnp.int32).astype(F32) * (2.0 * math.pi / NT)
    cos_off = jnp.cos(angle)[0:1, :]
    sin_off = jnp.sin(angle)[0:1, :]
    taper = 0.5 - 0.5 * (wave[0] * cos_off + wave[1] * sin_off)
    segment = jnp.concatenate(
        [centred[pl.ds(c, HIGH, stride=channels), :] * taper for c in range(channels)], axis=1
    )
    inner = jnp.dot(first[...], segment, precision=HIGHEST, preferred_element_type=F32)
    twist_cos, twist_sin = twist[0], twist[1]
    for c in range(channels):
        real = inner[:HIGH, c * LANES : (c + 1) * LANES]
        imag = inner[HIGH:, c * LANES : (c + 1) * LANES]
        real = jnp.concatenate([real, real], axis=0)
        imag = jnp.concatenate([imag, imag], axis=0)
        mixed = jnp.concatenate(
            [real * twist_cos - imag * twist_sin, real * twist_sin + imag * twist_cos], axis=1
        )
        bins = lax.dot_general(
            second[...],
            mixed,
            (((1,), (1,)), ((), ())),
            precision=HIGHEST,
            preferred_element_type=F32,
        )
        grid_real[pl.ds(c, GRID_ROWS, stride=channels), :] = bins[:GRID_ROWS]
        grid_imag[pl.ds(c, GRID_ROWS, stride=channels), :] = bins[GRID_ROWS:]

    live = (ROWS + 2) * channels
    real, imag = grid_real[:live, :], grid_imag[:live, :]
    power = (real * real + imag * imag) * (1.0 / (2 * SMOOTH_HALF + 1))
    place = lax.broadcasted_iota(jnp.int32, (channels, LANES), 1)
    head = jnp.where(place >= LANES - SMOOTH_HALF, power[:channels], 0.0)
    tail = jnp.where(place < SMOOTH_HALF, power[live - channels :], 0.0)
    power = jnp.concatenate([head, power[channels : live - channels], tail], axis=0)
    top, low = split(power)
    count = ROWS * channels
    around = [
        piece[i * channels : i * channels + count] for piece in (top, low) for i in range(3)
    ]
    level = jnp.dot(jnp.concatenate(around[:3], axis=1), band[...], preferred_element_type=F32)
    level += jnp.dot(jnp.concatenate(around[3:], axis=1), band[...], preferred_element_type=F32)
    scale = lax.rsqrt(level + 1e-06)
    kept_real = real[channels : channels + count] * scale
    kept_imag = imag[channels : channels + count] * scale
    part = ROWS // windows
    for i in range(ROWS):
        rows = slice(i * channels, (i + 1) * channels)
        tile = jnp.concatenate([kept_real[rows], kept_imag[rows]], axis=0).astype(BF16)
        white[i // part, :, (i % part) * LANES : (i % part + 1) * LANES] = tile
    for k in range(windows):
        outs[k][...] = white[me ^ k]
    fields = [f[...].astype(F32) for f in (source, receiver, hop, owner)]
    fields.append(jnp.zeros((2 * channels - 4, fields[0].shape[1]), F32))
    fields = jnp.concatenate(fields, axis=0)
    fields = jnp.concatenate(
        [fields, jnp.zeros((2 * channels, LANES - fields.shape[1]), F32)], axis=1
    )
    outs[windows][...] = fields.astype(BF16)


def stack_kernel(blocks, windows, capacity, reach, pair_slots, scalars, *rest):
    gathered, out = rest[:-1], rest[-1]
    me = scalars[0]
    height = gathered[0].shape[0]
    channels = height // 2
    width = (gathered[0].shape[1] - LANES) // windows
    slots = blocks * capacity
    meta = jnp.concatenate([g[:, windows * width :] for g in gathered], axis=0)

    row = lax.broadcasted_iota(jnp.int32, (slots, LANES), 0)
    lane = lax.broadcasted_iota(jnp.int32, (slots, LANES), 1)
    block = jnp.zeros((slots, LANES), jnp.int32)
    for b in range(1, blocks):
        block = block + (row >= b * capacity).astype(jnp.int32)
    slot = row - block * capacity

    def pick(index, size):
        spot = lax.broadcasted_iota(jnp.int32, (slots, size), 1)
        index = jnp.concatenate([index] * (size // LANES), axis=1)
        return jnp.where(spot == index, 1.0, 0.0).astype(BF16)

    base = (block ^ me) * height
    depth = blocks * height
    table = jnp.dot(
        jnp.concatenate([pick(base + i, depth) for i in range(4)], axis=0),
        meta,
        preferred_element_type=F32,
    )
    source, receiver, hop, owner = [table[i * slots : (i + 1) * slots] for i in range(4)]
    mine = jnp.where((owner == me.astype(F32)) & (lane < pair_slots), 1.0, 0.0)
    above = lax.broadcasted_iota(jnp.int32, (LANES, LANES), 0)
    below = lax.broadcasted_iota(jnp.int32, (LANES, LANES), 1)
    earlier = jnp.where(above < below, 1.0, 0.0).astype(BF16)
    rank = jnp.dot(mine.astype(BF16), earlier, preferred_element_type=F32)
    chosen = jnp.where(rank == slot.astype(F32), mine, 0.0)

    def value_of(field):
        return jnp.sum(chosen * field, axis=1, keepdims=True).astype(jnp.int32)

    filled = jnp.sum(chosen, axis=1, keepdims=True) > 0.5
    target = block + value_of(hop) - reach
    target = jnp.where(target < 0, target + blocks, target)
    target = jnp.where(target >= blocks, target - blocks, target)
    source_row = base + value_of(source)
    receiver_row = (target ^ me) * height + value_of(receiver)
    source_row = jnp.where(filled, source_row, -depth)
    receiver_row = jnp.where(filled, receiver_row, -depth)
    choice = jnp.concatenate(
        [
            pick(source_row, depth),
            pick(source_row + channels, depth),
            pick(receiver_row, depth),
            pick(receiver_row + channels, depth),
        ],
        axis=0,
    )
    real = jnp.zeros((slots, width), F32)
    imag = jnp.zeros((slots, width), F32)
    for w in range(windows):
        white = jnp.concatenate([g[:, w * width : (w + 1) * width] for g in gathered], axis=0)
        rows = jnp.dot(choice, white, preferred_element_type=F32)
        sr, si, rr, ri = [rows[i * slots : (i + 1) * slots] for i in range(4)]
        real += sr * rr + si * ri
        imag += sr * ri - si * rr
    parts = width // LANES
    for i in range(parts):
        lanes = slice(i * LANES, (i + 1) * LANES)
        out[pl.ds(2 * i, slots, stride=2 * parts), :] = real[:, lanes]
        out[pl.ds(2 * i + 1, slots, stride=2 * parts), :] = imag[:, lanes]


def swapped(value, axis, bits):
    peers = lax.axis_size(axis)
    return lax.ppermute(value, axis, [(i, i ^ bits) for i in range(peers)])


def local(traces, offsets, pair_source, pair_recv, pair_hop, pair_owner):
    blocks = lax.axis_size("chan")
    windows = lax.axis_size("win")
    channels = traces.shape[0]
    pair_slots = pair_source.shape[1]
    reach = min(8, (blocks - 1) // 2)
    capacity = 2 * ((pair_slots + blocks - 1) // blocks)
    width = F // windows
    vmem = pl.BlockSpec(memory_space=pltpu.VMEM)
    smem = pl.BlockSpec(memory_space=pltpu.SMEM)
    height = 2 * channels

    scalars = jnp.stack([offsets[0], lax.axis_index("win").astype(jnp.int32)])
    constants = [jnp.asarray(t) for t in tables()]
    pieces = pl.pallas_call(
        whiten_kernel,
        out_shape=[jax.ShapeDtypeStruct((height, width), BF16)] * windows
        + [jax.ShapeDtypeStruct((height, LANES), BF16)],
        in_specs=[smem] + [vmem] * 10,
        out_specs=[vmem] * (windows + 1),
        scratch_shapes=[
            pltpu.VMEM((HIGH * channels, LANES), F32),
            pltpu.VMEM((GRID_ROWS * channels, LANES), F32),
            pltpu.VMEM((GRID_ROWS * channels, LANES), F32),
            pltpu.VMEM((windows, height, width), BF16),
        ],
        compiler_params=pltpu.CompilerParams(vmem_limit_bytes=32 << 20),
        name="whiten",
    )(scalars, traces, pair_source, pair_recv, pair_hop, pair_owner.reshape(1, -1), *constants)
    moved = [pieces[0]] + [swapped(pieces[k], "win", k) for k in range(1, windows)]
    packed = jnp.concatenate(moved + [pieces[windows]], axis=1)

    gathered = {0: packed}
    for k in range(2, blocks, 2):
        gathered[k] = swapped(packed, "chan", k)
    for k in range(0, blocks, 2):
        gathered[k + 1] = swapped(gathered[k], "chan", 1)

    stacked = pl.pallas_call(
        functools.partial(stack_kernel, blocks, windows, capacity, reach, pair_slots),
        out_shape=jax.ShapeDtypeStruct((blocks * capacity * 2 * width // LANES, LANES), F32),
        in_specs=[smem] + [vmem] * blocks,
        out_specs=vmem,
        compiler_params=pltpu.CompilerParams(vmem_limit_bytes=32 << 20),
        name="stack",
    )(
        lax.axis_index("chan").astype(jnp.int32).reshape(1),
        *[gathered[k] for k in range(blocks)],
    )
    stacked = stacked.reshape(blocks * capacity, width // LANES, 2, LANES)
    return stacked.transpose(0, 2, 1, 3).reshape(blocks * capacity, 2, width)


def solution(mesh):
    placed = (
        P("chan", "win"),
        P("win"),
        P("chan", None),
        P("chan", None),
        P("chan", None),
        P("chan", None),
    )
    return jax.shard_map(
        local, mesh=mesh, in_specs=placed, out_specs=P("chan", None, "win"), check_vma=False
    )
```

```python
import functools
import math

import jax
import jax.numpy as jnp
import numpy as np
from jax import lax
from jax.experimental import pallas as pl
from jax.experimental.pallas import tpu as pltpu
from jax.sharding import PartitionSpec as P

NT = 8192
F = 2048
SMOOTH_HALF = 32
LANES = 128
HIGH = NT // LANES
ROWS = F // LANES
GRID_ROWS = 24
F32 = jnp.float32
BF16 = jnp.bfloat16
LIMIT = 55000 << 10


def tables():
    lane = np.arange(LANES)
    high = np.arange(HIGH)
    first = 2 * np.pi / HIGH * (np.outer(np.arange(HIGH) + SMOOTH_HALF, high) % HIGH)
    first = np.concatenate([np.cos(first), -np.sin(first)], axis=0)
    first = np.concatenate([first, first], axis=1)
    twist = 2 * np.pi / NT * (np.outer(lane + SMOOTH_HALF, lane) % NT)
    grid_row = np.arange(GRID_ROWS) - 1
    second = 2 * np.pi / HIGH * (np.outer(grid_row, lane) % HIGH)
    live = (np.arange(GRID_ROWS) < ROWS + 2)[:, None]
    cos, sin = np.cos(second) * live, -np.sin(second) * live
    phase = 2 * np.pi / NT * np.arange(NT).reshape(HIGH, LANES)
    rows = [np.cos(phase), np.sin(phase), first, np.cos(twist), -np.sin(twist), cos, sin]
    return np.concatenate(rows, axis=0).astype(np.float32)


def split(value):
    top = value.astype(BF16)
    return top, (value - top.astype(F32)).astype(BF16)


def whiten_kernel(place_ref, traces_far, offsets_far, table_far, *rest):
    outs = rest[:-9]
    traces, offsets, table, arrived, held, means, grid_real, grid_imag, white = rest[-9:]
    copies = [
        pltpu.make_async_copy(offsets_far, offsets, arrived.at[0]),
        pltpu.make_async_copy(traces_far, traces, arrived.at[1]),
        pltpu.make_async_copy(table_far, table, arrived.at[2]),
    ]
    for copy in copies:
        copy.start()
    windows = len(outs)
    channels = traces.shape[0]

    spot = lax.broadcasted_iota(jnp.int32, (3 * LANES, LANES), 0) - LANES
    spot = spot - lax.broadcasted_iota(jnp.int32, (3 * LANES, LANES), 1)
    band = jnp.where(jnp.abs(spot) <= SMOOTH_HALF, 1.0, 0.0).astype(BF16)

    copies[0].wait()
    offset, me = offsets[0], place_ref[0]
    copies[2].wait()
    place = lax.broadcasted_iota(jnp.int32, (1, LANES), 1) == offset % LANES
    turn = offset // LANES
    cos_off = jnp.sum(
        jnp.where(place, table[pl.ds(turn, 1), :], 0.0), axis=1, keepdims=True
    )
    sin_off = jnp.sum(
        jnp.where(place, table[pl.ds(HIGH + turn, 1), :], 0.0), axis=1, keepdims=True
    )
    taper = 0.5 - 0.5 * (table[:HIGH, :] * cos_off + table[HIGH : 2 * HIGH, :] * sin_off)
    at = 2 * HIGH
    first = split(table[at : at + 2 * HIGH, :HIGH])
    first = jnp.concatenate([first[0], first[0], first[1]], axis=1)
    at += 2 * HIGH
    twist_cos, twist_sin = table[at : at + LANES, :], table[at + LANES : at + 2 * LANES, :]
    at += 2 * LANES
    cos, sin = table[at : at + GRID_ROWS, :], table[at + GRID_ROWS : at + 2 * GRID_ROWS, :]
    second = split(
        jnp.concatenate(
            [jnp.concatenate([cos, -sin], axis=1), jnp.concatenate([sin, cos], axis=1)], axis=0
        )
    )
    second = jnp.concatenate([second[0], second[0], second[1]], axis=1)

    copies[1].wait()
    lane = lax.broadcasted_iota(jnp.int32, (channels, LANES), 1)
    totals = [jnp.zeros((channels, LANES), F32) for _ in range(4)]
    spare = traces.shape[1] // LANES - HIGH
    for i in range(HIGH):
        piece = traces[:, i * LANES : (i + 1) * LANES]
        if i < spare:
            later = traces[:, (i + HIGH) * LANES : (i + HIGH + 1) * LANES]
            piece = jnp.where(lane + i * LANES >= offset, piece, later)
        held[i * channels : (i + 1) * channels, :] = piece
        totals[i % 4] = totals[i % 4] + piece
    total = (totals[0] + totals[1]) + (totals[2] + totals[3])
    mean = jnp.sum(total, axis=1, keepdims=True) * (1.0 / NT)
    means[...] = jnp.broadcast_to(mean, (channels, LANES))
    segment = jnp.concatenate(
        [
            (held[pl.ds(c, HIGH, stride=channels), :] - means[c : c + 1, :]) * taper
            for c in range(channels)
        ],
        axis=1,
    )
    top, low = split(segment)
    inner = jnp.dot(
        first, jnp.concatenate([top, low, top], axis=0), preferred_element_type=F32
    )
    for c in range(channels):
        real = inner[:HIGH, c * LANES : (c + 1) * LANES]
        imag = inner[HIGH:, c * LANES : (c + 1) * LANES]
        real = jnp.concatenate([real, real], axis=0)
        imag = jnp.concatenate([imag, imag], axis=0)
        top, low = split(
            jnp.concatenate(
                [real * twist_cos - imag * twist_sin, real * twist_sin + imag * twist_cos],
                axis=1,
            )
        )
        bins = lax.dot_general(
            second,
            jnp.concatenate([top, low, top], axis=1),
            (((1,), (1,)), ((), ())),
            preferred_element_type=F32,
        )
        grid_real[pl.ds(c, GRID_ROWS, stride=channels), :] = bins[:GRID_ROWS]
        grid_imag[pl.ds(c, GRID_ROWS, stride=channels), :] = bins[GRID_ROWS:]

    live = (ROWS + 2) * channels
    real, imag = grid_real[:live, :], grid_imag[:live, :]
    power = (real * real + imag * imag) * (1.0 / (2 * SMOOTH_HALF + 1))
    head = jnp.where(lane >= LANES - SMOOTH_HALF, power[:channels], 0.0)
    tail = jnp.where(lane < SMOOTH_HALF, power[live - channels :], 0.0)
    power = jnp.concatenate([head, power[channels : live - channels], tail], axis=0)
    count = ROWS * channels
    level = jnp.zeros((count, LANES), F32)
    for part in split(power):
        around = [part[i * channels : i * channels + count] for i in range(3)]
        level += jnp.dot(jnp.concatenate(around, axis=1), band, preferred_element_type=F32)
    scale = lax.rsqrt(level + 1e-06)
    kept_real = real[channels : channels + count] * scale
    kept_imag = imag[channels : channels + count] * scale
    part = ROWS // windows
    for i in range(ROWS):
        rows = slice(i * channels, (i + 1) * channels)
        tile = jnp.concatenate([kept_real[rows], kept_imag[rows]], axis=0).astype(BF16)
        white[i // part, :, (i % part) * LANES : (i % part + 1) * LANES] = tile
    for k in range(windows):
        outs[k][...] = white[me ^ k]


def stack_kernel(blocks, windows, capacity, reach, pair_slots, scalars, *rest):
    gathered, out = rest[:-1], rest[-1]
    me = scalars[0]
    height = gathered[0].shape[0]
    channels = height // 2
    width = (gathered[0].shape[1] - LANES) // windows
    slots = blocks * capacity
    meta = jnp.concatenate([g[:, windows * width :] for g in gathered], axis=0)

    row = lax.broadcasted_iota(jnp.int32, (slots, LANES), 0)
    lane = lax.broadcasted_iota(jnp.int32, (slots, LANES), 1)
    block = jnp.zeros((slots, LANES), jnp.int32)
    for b in range(1, blocks):
        block = block + (row >= b * capacity).astype(jnp.int32)
    slot = row - block * capacity

    def pick(index, size):
        spot = lax.broadcasted_iota(jnp.int32, (slots, size), 1)
        index = jnp.concatenate([index] * (size // LANES), axis=1)
        return jnp.where(spot == index, 1.0, 0.0).astype(BF16)

    base = (block ^ me) * height
    depth = blocks * height
    table = jnp.dot(
        jnp.concatenate([pick(base + i, depth) for i in range(4)], axis=0),
        meta,
        preferred_element_type=F32,
    )
    source, receiver, hop, owner = [table[i * slots : (i + 1) * slots] for i in range(4)]
    mine = jnp.where((owner == me.astype(F32)) & (lane < pair_slots), 1.0, 0.0)
    above = lax.broadcasted_iota(jnp.int32, (LANES, LANES), 0)
    below = lax.broadcasted_iota(jnp.int32, (LANES, LANES), 1)
    earlier = jnp.where(above < below, 1.0, 0.0).astype(BF16)
    rank = jnp.dot(mine.astype(BF16), earlier, preferred_element_type=F32)
    chosen = jnp.where(rank == slot.astype(F32), mine, 0.0)

    def value_of(field):
        return jnp.sum(chosen * field, axis=1, keepdims=True).astype(jnp.int32)

    filled = jnp.sum(chosen, axis=1, keepdims=True) > 0.5
    target = block + value_of(hop) - reach
    target = jnp.where(target < 0, target + blocks, target)
    target = jnp.where(target >= blocks, target - blocks, target)
    source_row = base + value_of(source)
    receiver_row = (target ^ me) * height + value_of(receiver)
    source_row = jnp.where(filled, source_row, -depth)
    receiver_row = jnp.where(filled, receiver_row, -depth)
    choice = jnp.concatenate(
        [
            pick(source_row, depth),
            pick(source_row + channels, depth),
            pick(receiver_row, depth),
            pick(receiver_row + channels, depth),
        ],
        axis=0,
    )
    real = jnp.zeros((slots, width), F32)
    imag = jnp.zeros((slots, width), F32)
    for w in range(windows):
        white = jnp.concatenate([g[:, w * width : (w + 1) * width] for g in gathered], axis=0)
        rows = jnp.dot(choice, white, preferred_element_type=F32)
        sr, si, rr, ri = [rows[i * slots : (i + 1) * slots] for i in range(4)]
        real += sr * rr + si * ri
        imag += sr * ri - si * rr
    parts = width // LANES
    for i in range(parts):
        lanes = slice(i * LANES, (i + 1) * LANES)
        out[pl.ds(2 * i, slots, stride=2 * parts), :] = real[:, lanes]
        out[pl.ds(2 * i + 1, slots, stride=2 * parts), :] = imag[:, lanes]


def swapped(value, axis, bits):
    peers = lax.axis_size(axis)
    return lax.ppermute(value, axis, [(i, i ^ bits) for i in range(peers)])


def local(traces, offsets, pair_source, pair_recv, pair_hop, pair_owner):
    blocks = lax.axis_size("chan")
    windows = lax.axis_size("win")
    channels = traces.shape[0]
    pair_slots = pair_source.shape[1]
    reach = min(8, (blocks - 1) // 2)
    capacity = 2 * ((pair_slots + blocks - 1) // blocks)
    width = F // windows
    vmem = pl.BlockSpec(memory_space=pltpu.VMEM)
    smem = pl.BlockSpec(memory_space=pltpu.SMEM)
    height = 2 * channels

    table = jnp.asarray(tables())
    pieces = pl.pallas_call(
        whiten_kernel,
        out_shape=[jax.ShapeDtypeStruct((height, width), BF16)] * windows,
        in_specs=[smem] + [pl.BlockSpec(memory_space=pltpu.HBM)] * 3,
        out_specs=[vmem] * windows,
        scratch_shapes=[
            pltpu.VMEM(traces.shape, F32),
            pltpu.SMEM(offsets.shape, jnp.int32),
            pltpu.VMEM(table.shape, F32),
            pltpu.SemaphoreType.DMA((3,)),
            pltpu.VMEM((HIGH * channels, LANES), F32),
            pltpu.VMEM((channels, LANES), F32),
            pltpu.VMEM((GRID_ROWS * channels, LANES), F32),
            pltpu.VMEM((GRID_ROWS * channels, LANES), F32),
            pltpu.VMEM((windows, height, width), BF16),
        ],
        compiler_params=pltpu.CompilerParams(vmem_limit_bytes=LIMIT),
        name="whiten",
    )(lax.axis_index("win").astype(jnp.int32).reshape(1), traces, offsets, table)
    fields = [pair_source, pair_recv, pair_hop, pair_owner.reshape(1, -1)]
    fields = jnp.concatenate(fields, axis=0).astype(BF16)
    fields = jnp.pad(fields, ((0, height - 4), (0, LANES - pair_slots)))
    moved = [pieces[0]] + [swapped(pieces[k], "win", k) for k in range(1, windows)]
    packed = jnp.concatenate(moved + [fields], axis=1)

    gathered = {0: packed}
    half = blocks // 2
    for k in range(blocks - 2, half - 1, -2):
        gathered[k] = swapped(packed, "chan", k)
    for k in range(1, half):
        gathered[k] = swapped(packed, "chan", k)
    for k in range(blocks - 2, half - 1, -2):
        gathered[k + 1] = swapped(gathered[k], "chan", 1)

    stacked = pl.pallas_call(
        functools.partial(stack_kernel, blocks, windows, capacity, reach, pair_slots),
        out_shape=jax.ShapeDtypeStruct((blocks * capacity * 2 * width // LANES, LANES), F32),
        in_specs=[smem] + [vmem] * blocks,
        out_specs=vmem,
        compiler_params=pltpu.CompilerParams(vmem_limit_bytes=32 << 20),
        name="stack",
    )(
        lax.axis_index("chan").astype(jnp.int32).reshape(1),
        *[gathered[k] for k in range(blocks)],
    )
    stacked = stacked.reshape(blocks * capacity, width // LANES, 2, LANES)
    return stacked.transpose(0, 2, 1, 3).reshape(blocks * capacity, 2, width)


def solution(mesh):
    placed = (
        P("chan", "win"),
        P("win"),
        P("chan", None),
        P("chan", None),
        P("chan", None),
        P("chan", None),
    )
    return jax.shard_map(
        local, mesh=mesh, in_specs=placed, out_specs=P("chan", None, "win"), check_vma=False
    )
```

```python
import functools
import math

import jax
import jax.numpy as jnp
import numpy as np
from jax import lax
from jax.experimental import pallas as pl
from jax.experimental.pallas import tpu as pltpu
from jax.sharding import PartitionSpec as P

NT = 8192
F = 2048
SMOOTH_HALF = 32
LANES = 128
HIGH = NT // LANES
ROWS = F // LANES
GRID_ROWS = 24
F32 = jnp.float32
BF16 = jnp.bfloat16
LIMIT = 55000 << 10


def tables():
    lane = np.arange(LANES)
    high = np.arange(HIGH)
    first = 2 * np.pi / HIGH * (np.outer(np.arange(HIGH) + SMOOTH_HALF, high) % HIGH)
    first = np.concatenate([np.cos(first), -np.sin(first)], axis=0)
    first = np.concatenate([first, first], axis=1)
    twist = 2 * np.pi / NT * (np.outer(high + SMOOTH_HALF, lane) % NT)
    half_row = 2 * (np.arange(GRID_ROWS) - 1)
    half_row = np.concatenate([half_row, half_row + 1])
    second = 2 * np.pi / LANES * (np.outer(half_row, lane) % LANES)
    live = np.tile(np.arange(GRID_ROWS) < ROWS + 2, 2)[:, None]
    cos, sin = np.cos(second) * live, -np.sin(second) * live
    phase = 2 * np.pi / NT * np.arange(NT).reshape(HIGH, LANES)
    rows = [np.cos(phase), np.sin(phase), first, np.cos(twist), -np.sin(twist), cos, sin]
    return np.concatenate(rows, axis=0).astype(np.float32)


def split(value):
    top = value.astype(BF16)
    return top, (value - top.astype(F32)).astype(BF16)


def whiten_kernel(place_ref, traces_far, offsets_far, table_far, *rest):
    outs = rest[:-9]
    traces, offsets, table, arrived, held, means, grid_real, grid_imag, white = rest[-9:]
    copies = [
        pltpu.make_async_copy(offsets_far, offsets, arrived.at[0]),
        pltpu.make_async_copy(traces_far, traces, arrived.at[1]),
        pltpu.make_async_copy(table_far, table, arrived.at[2]),
    ]
    for copy in copies:
        copy.start()
    windows = len(outs)
    channels = traces.shape[0]

    spot = lax.broadcasted_iota(jnp.int32, (3 * LANES, LANES), 0) - LANES
    spot = spot - lax.broadcasted_iota(jnp.int32, (3 * LANES, LANES), 1)
    band = jnp.where(jnp.abs(spot) <= SMOOTH_HALF, 1.0, 0.0).astype(BF16)

    copies[0].wait()
    offset, me = offsets[0], place_ref[0]
    copies[2].wait()
    place = lax.broadcasted_iota(jnp.int32, (1, LANES), 1) == offset % LANES
    turn = offset // LANES
    cos_off = jnp.sum(
        jnp.where(place, table[pl.ds(turn, 1), :], 0.0), axis=1, keepdims=True
    )
    sin_off = jnp.sum(
        jnp.where(place, table[pl.ds(HIGH + turn, 1), :], 0.0), axis=1, keepdims=True
    )
    taper = 0.5 - 0.5 * (table[:HIGH, :] * cos_off + table[HIGH : 2 * HIGH, :] * sin_off)
    at = 2 * HIGH
    first = split(table[at : at + 2 * HIGH, :HIGH])
    first = jnp.concatenate([first[0], first[0], first[1]], axis=1)
    at += 2 * HIGH
    twist_cos = jnp.concatenate([table[at : at + HIGH, :]] * 2, axis=0)
    twist_sin = jnp.concatenate([table[at + HIGH : at + 2 * HIGH, :]] * 2, axis=0)
    at += 2 * HIGH
    cos, sin = table[at : at + 2 * GRID_ROWS, :], table[at + 2 * GRID_ROWS :, :]
    second = split(
        jnp.concatenate(
            [jnp.concatenate([cos, -sin], axis=1), jnp.concatenate([sin, cos], axis=1)], axis=0
        )
    )
    second = jnp.concatenate([second[0], second[0], second[1]], axis=1)

    copies[1].wait()
    lane = lax.broadcasted_iota(jnp.int32, (channels, LANES), 1)
    totals = [jnp.zeros((channels, LANES), F32) for _ in range(4)]
    spare = traces.shape[1] // LANES - HIGH
    for i in range(HIGH):
        piece = traces[:, i * LANES : (i + 1) * LANES]
        if i < spare:
            later = traces[:, (i + HIGH) * LANES : (i + HIGH + 1) * LANES]
            piece = jnp.where(lane + i * LANES >= offset, piece, later)
        held[i * channels : (i + 1) * channels, :] = piece
        totals[i % 4] = totals[i % 4] + piece
    total = (totals[0] + totals[1]) + (totals[2] + totals[3])
    mean = jnp.sum(total, axis=1, keepdims=True) * (1.0 / NT)
    means[...] = jnp.broadcast_to(mean, (channels, LANES))
    segment = jnp.concatenate(
        [
            (held[pl.ds(c, HIGH, stride=channels), :] - means[c : c + 1, :]) * taper
            for c in range(channels)
        ],
        axis=1,
    )
    top, low = split(segment)
    inner = jnp.dot(
        first, jnp.concatenate([top, low, top], axis=0), preferred_element_type=F32
    )
    lower = lax.broadcasted_iota(jnp.int32, (GRID_ROWS, LANES), 1) < HIGH
    mixed = []
    for c in range(0, channels, 2):
        pair = [slice((c + i) * LANES, (c + i + 1) * LANES) for i in range(2)]
        real = jnp.concatenate([inner[:HIGH, lanes] for lanes in pair], axis=0)
        imag = jnp.concatenate([inner[HIGH:, lanes] for lanes in pair], axis=0)
        top, low = split(
            jnp.concatenate(
                [real * twist_cos - imag * twist_sin, real * twist_sin + imag * twist_cos],
                axis=1,
            )
        )
        mixed.append(jnp.concatenate([top, low, top], axis=1))
    bins_of_all = lax.dot_general(
        second,
        jnp.concatenate(mixed, axis=0),
        (((1,), (1,)), ((), ())),
        preferred_element_type=F32,
    )
    for c in range(0, channels, 2):
        bins = bins_of_all[:, c // 2 * LANES : (c // 2 + 1) * LANES]
        for grid, start in ((grid_real, 0), (grid_imag, 2 * GRID_ROWS)):
            under = bins[start : start + GRID_ROWS]
            over = bins[start + GRID_ROWS : start + 2 * GRID_ROWS]
            rows = jnp.where(lower, under, pltpu.roll(over, HIGH, 1))
            grid[pl.ds(c, GRID_ROWS, stride=channels), :] = rows
            rows = jnp.where(lower, pltpu.roll(under, HIGH, 1), over)
            grid[pl.ds(c + 1, GRID_ROWS, stride=channels), :] = rows

    live = (ROWS + 2) * channels
    real, imag = grid_real[:live, :], grid_imag[:live, :]
    power = (real * real + imag * imag) * (1.0 / (2 * SMOOTH_HALF + 1))
    head = jnp.where(lane >= LANES - SMOOTH_HALF, power[:channels], 0.0)
    tail = jnp.where(lane < SMOOTH_HALF, power[live - channels :], 0.0)
    power = jnp.concatenate([head, power[channels : live - channels], tail], axis=0)
    count = ROWS * channels
    level = jnp.zeros((count, LANES), F32)
    for part in split(power):
        around = [part[i * channels : i * channels + count] for i in range(3)]
        level += jnp.dot(jnp.concatenate(around, axis=1), band, preferred_element_type=F32)
    scale = lax.rsqrt(level + 1e-06)
    kept_real = real[channels : channels + count] * scale
    kept_imag = imag[channels : channels + count] * scale
    part = ROWS // windows
    for i in range(ROWS):
        rows = slice(i * channels, (i + 1) * channels)
        tile = jnp.concatenate([kept_real[rows], kept_imag[rows]], axis=0).astype(BF16)
        white[i // part, :, (i % part) * LANES : (i % part + 1) * LANES] = tile
    for k in range(windows):
        outs[k][...] = white[me ^ k]


def stack_kernel(blocks, windows, capacity, reach, pair_slots, width, places, scalars, *rest):
    pieces, out = rest[:-1], rest[-1]
    me = scalars[0]
    height = pieces[0].shape[0]
    channels = height // 2
    slots = blocks * capacity

    def lanes_of(start, size):
        found = []
        for b in range(blocks):
            for index, offset in places[b]:
                if offset <= start < offset + pieces[index].shape[1]:
                    found.append(pieces[index][:, start - offset : start - offset + size])
        return jnp.concatenate(found, axis=0)

    meta = lanes_of(0, LANES)

    row = lax.broadcasted_iota(jnp.int32, (slots, LANES), 0)
    lane = lax.broadcasted_iota(jnp.int32, (slots, LANES), 1)
    block = jnp.zeros((slots, LANES), jnp.int32)
    for b in range(1, blocks):
        block = block + (row >= b * capacity).astype(jnp.int32)
    slot = row - block * capacity

    def pick(index, size):
        spot = lax.broadcasted_iota(jnp.int32, (slots, size), 1)
        index = jnp.concatenate([index] * (size // LANES), axis=1)
        return jnp.where(spot == index, 1.0, 0.0).astype(BF16)

    base = (block ^ me) * height
    depth = blocks * height
    table = jnp.dot(
        jnp.concatenate([pick(base + i, depth) for i in range(4)], axis=0),
        meta,
        preferred_element_type=F32,
    )
    source, receiver, hop, owner = [table[i * slots : (i + 1) * slots] for i in range(4)]
    mine = jnp.where((owner == me.astype(F32)) & (lane < pair_slots), 1.0, 0.0)
    above = lax.broadcasted_iota(jnp.int32, (LANES, LANES), 0)
    below = lax.broadcasted_iota(jnp.int32, (LANES, LANES), 1)
    earlier = jnp.where(above < below, 1.0, 0.0).astype(BF16)
    rank = jnp.dot(mine.astype(BF16), earlier, preferred_element_type=F32)
    chosen = jnp.where(rank == slot.astype(F32), mine, 0.0)

    def value_of(field):
        return jnp.sum(chosen * field, axis=1, keepdims=True).astype(jnp.int32)

    filled = jnp.sum(chosen, axis=1, keepdims=True) > 0.5
    target = block + value_of(hop) - reach
    target = jnp.where(target < 0, target + blocks, target)
    target = jnp.where(target >= blocks, target - blocks, target)
    source_row = base + value_of(source)
    receiver_row = (target ^ me) * height + value_of(receiver)
    source_row = jnp.where(filled, source_row, -depth)
    receiver_row = jnp.where(filled, receiver_row, -depth)
    choice = jnp.concatenate(
        [
            pick(source_row, depth),
            pick(source_row + channels, depth),
            pick(receiver_row, depth),
            pick(receiver_row + channels, depth),
        ],
        axis=0,
    )
    real = jnp.zeros((slots, width), F32)
    imag = jnp.zeros((slots, width), F32)
    for w in range(windows):
        white = lanes_of(LANES + w * width, width)
        rows = jnp.dot(choice, white, preferred_element_type=F32)
        sr, si, rr, ri = [rows[i * slots : (i + 1) * slots] for i in range(4)]
        real += sr * rr + si * ri
        imag += sr * ri - si * rr
    parts = width // LANES
    for i in range(parts):
        lanes = slice(i * LANES, (i + 1) * LANES)
        out[pl.ds(2 * i, slots, stride=2 * parts), :] = real[:, lanes]
        out[pl.ds(2 * i + 1, slots, stride=2 * parts), :] = imag[:, lanes]


def swapped(value, axis, bits):
    peers = lax.axis_size(axis)
    return lax.ppermute(value, axis, [(i, i ^ bits) for i in range(peers)])


def local(traces, offsets, pair_source, pair_recv, pair_hop, pair_owner):
    blocks = lax.axis_size("chan")
    windows = lax.axis_size("win")
    channels = traces.shape[0]
    pair_slots = pair_source.shape[1]
    reach = min(8, (blocks - 1) // 2)
    capacity = 2 * ((pair_slots + blocks - 1) // blocks)
    width = F // windows
    vmem = pl.BlockSpec(memory_space=pltpu.VMEM)
    smem = pl.BlockSpec(memory_space=pltpu.SMEM)
    height = 2 * channels

    table = jnp.asarray(tables())
    pieces = pl.pallas_call(
        whiten_kernel,
        out_shape=[jax.ShapeDtypeStruct((height, width), BF16)] * windows,
        in_specs=[smem] + [pl.BlockSpec(memory_space=pltpu.HBM)] * 3,
        out_specs=[vmem] * windows,
        scratch_shapes=[
            pltpu.VMEM(traces.shape, F32),
            pltpu.SMEM(offsets.shape, jnp.int32),
            pltpu.VMEM(table.shape, F32),
            pltpu.SemaphoreType.DMA((3,)),
            pltpu.VMEM((HIGH * channels, LANES), F32),
            pltpu.VMEM((channels, LANES), F32),
            pltpu.VMEM((GRID_ROWS * channels, LANES), F32),
            pltpu.VMEM((GRID_ROWS * channels, LANES), F32),
            pltpu.VMEM((windows, height, width), BF16),
        ],
        compiler_params=pltpu.CompilerParams(vmem_limit_bytes=LIMIT),
        name="whiten",
    )(lax.axis_index("win").astype(jnp.int32).reshape(1), traces, offsets, table)
    fields = [pair_source, pair_recv, pair_hop, pair_owner.reshape(1, -1)]
    fields = sum(
        jnp.pad(field, ((i, height - 1 - i), (0, LANES - pair_slots)))
        for i, field in enumerate(fields)
    ).astype(BF16)
    moved = [pieces[0]] + [swapped(pieces[k], "win", k) for k in range(windows - 1, 0, -1)]
    packed = jnp.concatenate([fields] + moved, axis=1)

    gathered = {0: [packed]}
    half = blocks // 2
    for k in range(blocks - 2, half - 1, -2):
        gathered[k] = [swapped(packed, "chan", k)]
    for k in range(1, half):
        gathered[k] = [swapped(packed, "chan", k)]
    for k in range(blocks - 2, half - 1, -2):
        gathered[k + 1] = [swapped(piece, "chan", 1) for piece in gathered[k]]

    order = [k for k in range(blocks - 2, half - 1, -2)]
    order = [k + i for k in order for i in range(2)] + list(range(half - 1, -1, -1))
    operands, places = [], {}
    for k in order:
        offset, places[k] = 0, []
        for piece in gathered[k]:
            places[k].append((len(operands), offset))
            operands.append(piece)
            offset += piece.shape[1]

    stacked = pl.pallas_call(
        functools.partial(
            stack_kernel, blocks, windows, capacity, reach, pair_slots, width, places
        ),
        out_shape=jax.ShapeDtypeStruct((blocks * capacity * 2 * width // LANES, LANES), F32),
        in_specs=[smem] + [vmem] * len(operands),
        out_specs=vmem,
        compiler_params=pltpu.CompilerParams(vmem_limit_bytes=32 << 20),
        name="stack",
    )(lax.axis_index("chan").astype(jnp.int32).reshape(1), *operands)
    stacked = stacked.reshape(blocks * capacity, width // LANES, 2, LANES)
    return stacked.transpose(0, 2, 1, 3).reshape(blocks * capacity, 2, width)


def solution(mesh):
    placed = (
        P("chan", "win"),
        P("win"),
        P("chan", None),
        P("chan", None),
        P("chan", None),
        P("chan", None),
    )
    return jax.shard_map(
        local, mesh=mesh, in_specs=placed, out_specs=P("chan", None, "win"), check_vma=False
    )
```

```python
import functools
import math

import jax
import jax.numpy as jnp
import numpy as np
from jax import lax
from jax.experimental import pallas as pl
from jax.experimental.pallas import tpu as pltpu
from jax.sharding import PartitionSpec as P

NT = 8192
F = 2048
SMOOTH_HALF = 32
LANES = 128
HIGH = NT // LANES
ROWS = F // LANES
GRID_ROWS = 24
F32 = jnp.float32
BF16 = jnp.bfloat16
LIMIT = 55000 << 10


def tables():
    lane = np.arange(LANES)
    high = np.arange(HIGH)
    first = 2 * np.pi / HIGH * (np.outer(np.arange(HIGH) + SMOOTH_HALF, high) % HIGH)
    first = np.concatenate([np.cos(first), -np.sin(first)], axis=0)
    first = np.concatenate([first, first], axis=1)
    twist = 2 * np.pi / NT * (np.outer(high + SMOOTH_HALF, lane) % NT)
    half_row = 2 * (np.arange(GRID_ROWS) - 1)
    half_row = np.concatenate([half_row, half_row + 1])
    second = 2 * np.pi / LANES * (np.outer(half_row, lane) % LANES)
    live = np.tile(np.arange(GRID_ROWS) < ROWS + 2, 2)[:, None]
    cos, sin = np.cos(second) * live, -np.sin(second) * live
    phase = 2 * np.pi / NT * np.arange(NT).reshape(HIGH, LANES)
    rows = [np.cos(phase), np.sin(phase), first, np.cos(twist), -np.sin(twist), cos, sin]
    return np.concatenate(rows, axis=0).astype(np.float32)


def split(value):
    top = value.astype(BF16)
    return top, (value - top.astype(F32)).astype(BF16)


def whiten_kernel(place_ref, traces_far, offsets_far, table_far, *rest):
    outs = rest[:-9]
    traces, offsets, table, arrived, held, means, grid_real, grid_imag, white = rest[-9:]
    copies = [
        pltpu.make_async_copy(offsets_far, offsets, arrived.at[0]),
        pltpu.make_async_copy(traces_far, traces, arrived.at[1]),
        pltpu.make_async_copy(table_far, table, arrived.at[2]),
    ]
    for copy in copies:
        copy.start()
    windows = len(outs)
    channels = traces.shape[0]

    spot = lax.broadcasted_iota(jnp.int32, (3 * LANES, LANES), 0) - LANES
    spot = spot - lax.broadcasted_iota(jnp.int32, (3 * LANES, LANES), 1)
    band = jnp.where(jnp.abs(spot) <= SMOOTH_HALF, 1.0, 0.0).astype(BF16)

    copies[0].wait()
    offset, me = offsets[0], place_ref[0]
    copies[2].wait()
    place = lax.broadcasted_iota(jnp.int32, (1, LANES), 1) == offset % LANES
    turn = offset // LANES
    cos_off = jnp.sum(
        jnp.where(place, table[pl.ds(turn, 1), :], 0.0), axis=1, keepdims=True
    )
    sin_off = jnp.sum(
        jnp.where(place, table[pl.ds(HIGH + turn, 1), :], 0.0), axis=1, keepdims=True
    )
    taper = 0.5 - 0.5 * (table[:HIGH, :] * cos_off + table[HIGH : 2 * HIGH, :] * sin_off)
    at = 2 * HIGH
    first = split(table[at : at + 2 * HIGH, :HIGH])
    first = jnp.concatenate([first[0], first[0], first[1]], axis=1)
    at += 2 * HIGH
    twist_cos = jnp.concatenate([table[at : at + HIGH, :]] * 2, axis=0)
    twist_sin = jnp.concatenate([table[at + HIGH : at + 2 * HIGH, :]] * 2, axis=0)
    at += 2 * HIGH
    cos, sin = table[at : at + 2 * GRID_ROWS, :], table[at + 2 * GRID_ROWS :, :]
    second = split(
        jnp.concatenate(
            [jnp.concatenate([cos, -sin], axis=1), jnp.concatenate([sin, cos], axis=1)], axis=0
        )
    )
    second = jnp.concatenate([second[0], second[0], second[1]], axis=1)

    copies[1].wait()
    lane = lax.broadcasted_iota(jnp.int32, (channels, LANES), 1)
    totals = [jnp.zeros((channels, LANES), F32) for _ in range(4)]
    spare = traces.shape[1] // LANES - HIGH
    for i in range(HIGH):
        piece = traces[:, i * LANES : (i + 1) * LANES]
        if i < spare:
            later = traces[:, (i + HIGH) * LANES : (i + HIGH + 1) * LANES]
            piece = jnp.where(lane + i * LANES >= offset, piece, later)
        held[i * channels : (i + 1) * channels, :] = piece
        totals[i % 4] = totals[i % 4] + piece
    total = (totals[0] + totals[1]) + (totals[2] + totals[3])
    mean = jnp.sum(total, axis=1, keepdims=True) * (1.0 / NT)
    means[...] = jnp.broadcast_to(mean, (channels, LANES))
    segment = jnp.concatenate(
        [
            (held[pl.ds(c, HIGH, stride=channels), :] - means[c : c + 1, :]) * taper
            for c in range(channels)
        ],
        axis=1,
    )
    top, low = split(segment)
    inner = jnp.dot(
        first, jnp.concatenate([top, low, top], axis=0), preferred_element_type=F32
    )
    lower = lax.broadcasted_iota(jnp.int32, (GRID_ROWS, LANES), 1) < HIGH
    mixed = []
    for c in range(0, channels, 2):
        pair = [slice((c + i) * LANES, (c + i + 1) * LANES) for i in range(2)]
        real = jnp.concatenate([inner[:HIGH, lanes] for lanes in pair], axis=0)
        imag = jnp.concatenate([inner[HIGH:, lanes] for lanes in pair], axis=0)
        top, low = split(
            jnp.concatenate(
                [real * twist_cos - imag * twist_sin, real * twist_sin + imag * twist_cos],
                axis=1,
            )
        )
        mixed.append(jnp.concatenate([top, low, top], axis=1))
    bins_of_all = lax.dot_general(
        second,
        jnp.concatenate(mixed, axis=0),
        (((1,), (1,)), ((), ())),
        preferred_element_type=F32,
    )
    for c in range(0, channels, 2):
        bins = bins_of_all[:, c // 2 * LANES : (c // 2 + 1) * LANES]
        for grid, start in ((grid_real, 0), (grid_imag, 2 * GRID_ROWS)):
            under = bins[start : start + GRID_ROWS]
            over = bins[start + GRID_ROWS : start + 2 * GRID_ROWS]
            rows = jnp.where(lower, under, pltpu.roll(over, HIGH, 1))
            grid[pl.ds(c, GRID_ROWS, stride=channels), :] = rows
            rows = jnp.where(lower, pltpu.roll(under, HIGH, 1), over)
            grid[pl.ds(c + 1, GRID_ROWS, stride=channels), :] = rows

    live = (ROWS + 2) * channels
    real, imag = grid_real[:live, :], grid_imag[:live, :]
    power = (real * real + imag * imag) * (1.0 / (2 * SMOOTH_HALF + 1))
    head = jnp.where(lane >= LANES - SMOOTH_HALF, power[:channels], 0.0)
    tail = jnp.where(lane < SMOOTH_HALF, power[live - channels :], 0.0)
    power = jnp.concatenate([head, power[channels : live - channels], tail], axis=0)
    count = ROWS * channels
    level = jnp.zeros((count, LANES), F32)
    for part in split(power):
        around = [part[i * channels : i * channels + count] for i in range(3)]
        level += jnp.dot(jnp.concatenate(around, axis=1), band, preferred_element_type=F32)
    scale = lax.rsqrt(level + 1e-06)
    kept_real = real[channels : channels + count] * scale
    kept_imag = imag[channels : channels + count] * scale
    part = ROWS // windows
    for i in range(ROWS):
        rows = slice(i * channels, (i + 1) * channels)
        tile = jnp.concatenate([kept_real[rows], kept_imag[rows]], axis=0).astype(BF16)
        white[i // part, :, (i % part) * LANES : (i % part + 1) * LANES] = tile
    for k in range(windows):
        outs[k][...] = white[me ^ k]


def stack_kernel(blocks, windows, capacity, reach, pair_slots, width, order, scalars, *rest):
    pieces, out = rest[:-1], rest[-1]
    me = scalars[0]
    height = pieces[0].shape[0]
    channels = height // 2
    slots = blocks * capacity

    def lanes_of(start, size):
        return jnp.concatenate(
            [pieces[order.index(b)][:, start : start + size] for b in range(blocks)], axis=0
        )

    meta = lanes_of(0, LANES)

    row = lax.broadcasted_iota(jnp.int32, (slots, LANES), 0)
    lane = lax.broadcasted_iota(jnp.int32, (slots, LANES), 1)
    block = jnp.zeros((slots, LANES), jnp.int32)
    for b in range(1, blocks):
        block = block + (row >= b * capacity).astype(jnp.int32)
    slot = row - block * capacity

    def pick(index, size):
        spot = lax.broadcasted_iota(jnp.int32, (slots, size), 1)
        index = jnp.concatenate([index] * (size // LANES), axis=1)
        return jnp.where(spot == index, 1.0, 0.0).astype(BF16)

    base = (block ^ me) * height
    depth = blocks * height
    table = jnp.dot(
        jnp.concatenate([pick(base + i, depth) for i in range(4)], axis=0),
        meta,
        preferred_element_type=F32,
    )
    source, receiver, hop, owner = [table[i * slots : (i + 1) * slots] for i in range(4)]
    mine = jnp.where((owner == me.astype(F32)) & (lane < pair_slots), 1.0, 0.0)
    above = lax.broadcasted_iota(jnp.int32, (LANES, LANES), 0)
    below = lax.broadcasted_iota(jnp.int32, (LANES, LANES), 1)
    earlier = jnp.where(above < below, 1.0, 0.0).astype(BF16)
    rank = jnp.dot(mine.astype(BF16), earlier, preferred_element_type=F32)
    chosen = jnp.where(rank == slot.astype(F32), mine, 0.0)

    def value_of(field):
        return jnp.sum(chosen * field, axis=1, keepdims=True).astype(jnp.int32)

    filled = jnp.sum(chosen, axis=1, keepdims=True) > 0.5
    target = block + value_of(hop) - reach
    target = jnp.where(target < 0, target + blocks, target)
    target = jnp.where(target >= blocks, target - blocks, target)
    source_row = base + value_of(source)
    receiver_row = (target ^ me) * height + value_of(receiver)
    source_row = jnp.where(filled, source_row, -depth)
    receiver_row = jnp.where(filled, receiver_row, -depth)
    choice = jnp.concatenate(
        [
            pick(source_row, depth),
            pick(source_row + channels, depth),
            pick(receiver_row, depth),
            pick(receiver_row + channels, depth),
        ],
        axis=0,
    )
    real = jnp.zeros((slots, width), F32)
    imag = jnp.zeros((slots, width), F32)
    for w in range(windows):
        white = lanes_of(LANES + w * width, width)
        rows = jnp.dot(choice, white, preferred_element_type=F32)
        sr, si, rr, ri = [rows[i * slots : (i + 1) * slots] for i in range(4)]
        real += sr * rr + si * ri
        imag += sr * ri - si * rr
    parts = width // LANES
    for i in range(parts):
        lanes = slice(i * LANES, (i + 1) * LANES)
        out[pl.ds(2 * i, slots, stride=2 * parts), :] = real[:, lanes]
        out[pl.ds(2 * i + 1, slots, stride=2 * parts), :] = imag[:, lanes]


def swapped(value, axis, bits):
    peers = lax.axis_size(axis)
    return lax.ppermute(value, axis, [(i, i ^ bits) for i in range(peers)])


def local(traces, offsets, pair_source, pair_recv, pair_hop, pair_owner):
    blocks = lax.axis_size("chan")
    windows = lax.axis_size("win")
    channels = traces.shape[0]
    pair_slots = pair_source.shape[1]
    reach = min(8, (blocks - 1) // 2)
    capacity = 2 * ((pair_slots + blocks - 1) // blocks)
    width = F // windows
    vmem = pl.BlockSpec(memory_space=pltpu.VMEM)
    smem = pl.BlockSpec(memory_space=pltpu.SMEM)
    height = 2 * channels

    table = jnp.asarray(tables())
    pieces = pl.pallas_call(
        whiten_kernel,
        out_shape=[jax.ShapeDtypeStruct((height, width), BF16)] * windows,
        in_specs=[smem] + [pl.BlockSpec(memory_space=pltpu.HBM)] * 3,
        out_specs=[vmem] * windows,
        scratch_shapes=[
            pltpu.VMEM(traces.shape, F32),
            pltpu.SMEM(offsets.shape, jnp.int32),
            pltpu.VMEM(table.shape, F32),
            pltpu.SemaphoreType.DMA((3,)),
            pltpu.VMEM((HIGH * channels, LANES), F32),
            pltpu.VMEM((channels, LANES), F32),
            pltpu.VMEM((GRID_ROWS * channels, LANES), F32),
            pltpu.VMEM((GRID_ROWS * channels, LANES), F32),
            pltpu.VMEM((windows, height, width), BF16),
        ],
        compiler_params=pltpu.CompilerParams(vmem_limit_bytes=LIMIT),
        name="whiten",
    )(lax.axis_index("win").astype(jnp.int32).reshape(1), traces, offsets, table)
    fields = [pair_source, pair_recv, pair_hop, pair_owner.reshape(1, -1)]
    fields = sum(
        jnp.pad(field, ((i, height - 1 - i), (0, LANES - pair_slots)))
        for i, field in enumerate(fields)
    ).astype(BF16)
    moved = [pieces[0]] + [swapped(pieces[k], "win", k) for k in range(windows - 1, 0, -1)]
    packed = jnp.concatenate([fields] + moved, axis=1)

    gathered = {0: packed}
    roots = [k + 2 for k in range(4, blocks, 4)]
    for root in roots:
        gathered[root] = swapped(packed, "chan", root)
    for k in range(1, 4):
        gathered[k] = swapped(packed, "chan", k)
    for root in roots:
        for k in range(1, 4):
            gathered[root ^ k] = swapped(gathered[root], "chan", k)
    order = [root ^ k for root in roots for k in (2, 1, 3, 0)] + [3, 2, 1, 0]

    stacked = pl.pallas_call(
        functools.partial(
            stack_kernel, blocks, windows, capacity, reach, pair_slots, width, order
        ),
        out_shape=jax.ShapeDtypeStruct((blocks * capacity * 2 * width // LANES, LANES), F32),
        in_specs=[smem] + [vmem] * blocks,
        out_specs=vmem,
        compiler_params=pltpu.CompilerParams(vmem_limit_bytes=32 << 20),
        name="stack",
    )(lax.axis_index("chan").astype(jnp.int32).reshape(1), *[gathered[k] for k in order])
    stacked = stacked.reshape(blocks * capacity, width // LANES, 2, LANES)
    return stacked.transpose(0, 2, 1, 3).reshape(blocks * capacity, 2, width)


def solution(mesh):
    placed = (
        P("chan", "win"),
        P("win"),
        P("chan", None),
        P("chan", None),
        P("chan", None),
        P("chan", None),
    )
    return jax.shard_map(
        local, mesh=mesh, in_specs=placed, out_specs=P("chan", None, "win"), check_vma=False
    )
```

```python
import functools
import math

import jax
import jax.numpy as jnp
import numpy as np
from jax import lax
from jax.experimental import pallas as pl
from jax.experimental.pallas import tpu as pltpu
from jax.sharding import PartitionSpec as P

NT = 8192
F = 2048
SMOOTH_HALF = 32
LANES = 128
HIGH = NT // LANES
ROWS = F // LANES
GRID_ROWS = 24
F32 = jnp.float32
BF16 = jnp.bfloat16
LIMIT = 55000 << 10


def tables():
    lane = np.arange(LANES)
    high = np.arange(HIGH)
    first = 2 * np.pi / HIGH * (np.outer(np.arange(HIGH) + SMOOTH_HALF, high) % HIGH)
    first = np.concatenate([np.cos(first), -np.sin(first)], axis=0)
    first = np.concatenate([first, first], axis=1)
    twist = 2 * np.pi / NT * (np.outer(high + SMOOTH_HALF, lane) % NT)
    half_row = 2 * (np.arange(GRID_ROWS) - 1)
    half_row = np.concatenate([half_row, half_row + 1])
    second = 2 * np.pi / LANES * (np.outer(half_row, lane) % LANES)
    live = np.tile(np.arange(GRID_ROWS) < ROWS + 2, 2)[:, None]
    cos, sin = np.cos(second) * live, -np.sin(second) * live
    phase = 2 * np.pi / NT * np.arange(NT).reshape(HIGH, LANES)
    rows = [np.cos(phase), np.sin(phase), first, np.cos(twist), -np.sin(twist), cos, sin]
    return np.concatenate(rows, axis=0).astype(np.float32)


def split(value):
    top = value.astype(BF16)
    return top, (value - top.astype(F32)).astype(BF16)


def whiten_kernel(place_ref, traces_far, offsets_far, table_far, *rest):
    outs = rest[:-9]
    traces, offsets, table, arrived, held, means, grid_real, grid_imag, white = rest[-9:]
    copies = [
        pltpu.make_async_copy(offsets_far, offsets, arrived.at[0]),
        pltpu.make_async_copy(traces_far, traces, arrived.at[1]),
        pltpu.make_async_copy(table_far, table, arrived.at[2]),
    ]
    for copy in copies:
        copy.start()
    windows = len(outs)
    channels = traces.shape[0]

    spot = lax.broadcasted_iota(jnp.int32, (3 * LANES, LANES), 0) - LANES
    spot = spot - lax.broadcasted_iota(jnp.int32, (3 * LANES, LANES), 1)
    band = jnp.where(jnp.abs(spot) <= SMOOTH_HALF, 1.0, 0.0).astype(BF16)

    copies[0].wait()
    offset, me = offsets[0], place_ref[0]
    copies[2].wait()
    place = lax.broadcasted_iota(jnp.int32, (1, LANES), 1) == offset % LANES
    turn = offset // LANES
    cos_off = jnp.sum(
        jnp.where(place, table[pl.ds(turn, 1), :], 0.0), axis=1, keepdims=True
    )
    sin_off = jnp.sum(
        jnp.where(place, table[pl.ds(HIGH + turn, 1), :], 0.0), axis=1, keepdims=True
    )
    taper = 0.5 - 0.5 * (table[:HIGH, :] * cos_off + table[HIGH : 2 * HIGH, :] * sin_off)
    at = 2 * HIGH
    first = split(table[at : at + 2 * HIGH, :HIGH])
    first = jnp.concatenate([first[0], first[0], first[1]], axis=1)
    at += 2 * HIGH
    twist_cos = jnp.concatenate([table[at : at + HIGH, :]] * 2, axis=0)
    twist_sin = jnp.concatenate([table[at + HIGH : at + 2 * HIGH, :]] * 2, axis=0)
    at += 2 * HIGH
    cos, sin = table[at : at + 2 * GRID_ROWS, :], table[at + 2 * GRID_ROWS :, :]
    second = split(
        jnp.concatenate(
            [jnp.concatenate([cos, -sin], axis=1), jnp.concatenate([sin, cos], axis=1)], axis=0
        )
    )
    second = jnp.concatenate([second[0], second[0], second[1]], axis=1)

    copies[1].wait()
    lane = lax.broadcasted_iota(jnp.int32, (channels, LANES), 1)
    totals = [jnp.zeros((channels, LANES), F32) for _ in range(4)]
    spare = traces.shape[1] // LANES - HIGH
    for i in range(HIGH):
        piece = traces[:, i * LANES : (i + 1) * LANES]
        if i < spare:
            later = traces[:, (i + HIGH) * LANES : (i + HIGH + 1) * LANES]
            piece = jnp.where(lane + i * LANES >= offset, piece, later)
        held[i * channels : (i + 1) * channels, :] = piece
        totals[i % 4] = totals[i % 4] + piece
    total = (totals[0] + totals[1]) + (totals[2] + totals[3])
    mean = jnp.sum(total, axis=1, keepdims=True) * (1.0 / NT)
    means[...] = jnp.broadcast_to(mean, (channels, LANES))
    inner = []
    for c in range(0, channels, 2):
        segment = [
            (held[pl.ds(c + i, HIGH, stride=channels), :] - means[c + i : c + i + 1, :]) * taper
            for i in range(2)
        ]
        top, low = split(jnp.concatenate(segment, axis=1))
        stacked = jnp.concatenate([top, low, top], axis=0)
        inner.append(jnp.dot(first, stacked, preferred_element_type=F32))
    inner = jnp.concatenate(inner, axis=1)
    lower = lax.broadcasted_iota(jnp.int32, (GRID_ROWS, LANES), 1) < HIGH
    mixed = []
    for c in range(0, channels, 2):
        pair = [slice((c + i) * LANES, (c + i + 1) * LANES) for i in range(2)]
        real = jnp.concatenate([inner[:HIGH, lanes] for lanes in pair], axis=0)
        imag = jnp.concatenate([inner[HIGH:, lanes] for lanes in pair], axis=0)
        top, low = split(
            jnp.concatenate(
                [real * twist_cos - imag * twist_sin, real * twist_sin + imag * twist_cos],
                axis=1,
            )
        )
        mixed.append(jnp.concatenate([top, low, top], axis=1))
    bins_of_all = lax.dot_general(
        second,
        jnp.concatenate(mixed, axis=0),
        (((1,), (1,)), ((), ())),
        preferred_element_type=F32,
    )
    for c in range(0, channels, 2):
        bins = bins_of_all[:, c // 2 * LANES : (c // 2 + 1) * LANES]
        for grid, start in ((grid_real, 0), (grid_imag, 2 * GRID_ROWS)):
            under = bins[start : start + GRID_ROWS]
            over = bins[start + GRID_ROWS : start + 2 * GRID_ROWS]
            rows = jnp.where(lower, under, pltpu.roll(over, HIGH, 1))
            grid[pl.ds(c, GRID_ROWS, stride=channels), :] = rows
            rows = jnp.where(lower, pltpu.roll(under, HIGH, 1), over)
            grid[pl.ds(c + 1, GRID_ROWS, stride=channels), :] = rows

    live = (ROWS + 2) * channels
    real, imag = grid_real[:live, :], grid_imag[:live, :]
    power = (real * real + imag * imag) * (1.0 / (2 * SMOOTH_HALF + 1))
    head = jnp.where(lane >= LANES - SMOOTH_HALF, power[:channels], 0.0)
    tail = jnp.where(lane < SMOOTH_HALF, power[live - channels :], 0.0)
    power = jnp.concatenate([head, power[channels : live - channels], tail], axis=0)
    count = ROWS * channels
    level = jnp.zeros((count, LANES), F32)
    for part in split(power):
        around = [part[i * channels : i * channels + count] for i in range(3)]
        level += jnp.dot(jnp.concatenate(around, axis=1), band, preferred_element_type=F32)
    scale = lax.rsqrt(level + 1e-06)
    kept_real = real[channels : channels + count] * scale
    kept_imag = imag[channels : channels + count] * scale
    part = ROWS // windows
    for i in range(ROWS):
        rows = slice(i * channels, (i + 1) * channels)
        tile = jnp.concatenate([kept_real[rows], kept_imag[rows]], axis=0).astype(BF16)
        white[i // part, :, (i % part) * LANES : (i % part + 1) * LANES] = tile
    for k in range(windows):
        outs[k][...] = white[me ^ k]


def stack_kernel(blocks, windows, capacity, reach, pair_slots, width, order, scalars, *rest):
    pieces, out = rest[:-1], rest[-1]
    me = scalars[0]
    height = pieces[0].shape[0]
    channels = height // 2
    slots = blocks * capacity

    def lanes_of(start, size):
        return jnp.concatenate(
            [pieces[order.index(b)][:, start : start + size] for b in range(blocks)], axis=0
        )

    meta = lanes_of(0, LANES)

    row = lax.broadcasted_iota(jnp.int32, (slots, LANES), 0)
    lane = lax.broadcasted_iota(jnp.int32, (slots, LANES), 1)
    block = jnp.zeros((slots, LANES), jnp.int32)
    for b in range(1, blocks):
        block = block + (row >= b * capacity).astype(jnp.int32)
    slot = row - block * capacity

    def pick(index, size):
        spot = lax.broadcasted_iota(jnp.int32, (slots, size), 1)
        index = jnp.concatenate([index] * (size // LANES), axis=1)
        return jnp.where(spot == index, 1.0, 0.0).astype(BF16)

    base = (block ^ me) * height
    depth = blocks * height
    table = jnp.dot(
        jnp.concatenate([pick(base + i, depth) for i in range(4)], axis=0),
        meta,
        preferred_element_type=F32,
    )
    source, receiver, hop, target_row = [table[i * slots : (i + 1) * slots] for i in range(4)]
    wanted = (me * capacity + slot).astype(F32)
    chosen = jnp.where((target_row == wanted) & (lane < pair_slots), 1.0, 0.0)

    def value_of(field):
        return jnp.sum(chosen * field, axis=1, keepdims=True).astype(jnp.int32)

    filled = jnp.sum(chosen, axis=1, keepdims=True) > 0.5
    target = block + value_of(hop) - reach
    target = jnp.where(target < 0, target + blocks, target)
    target = jnp.where(target >= blocks, target - blocks, target)
    source_row = base + value_of(source)
    receiver_row = (target ^ me) * height + value_of(receiver)
    source_row = jnp.where(filled, source_row, -depth)
    receiver_row = jnp.where(filled, receiver_row, -depth)
    choice = jnp.concatenate(
        [
            pick(source_row, depth),
            pick(source_row + channels, depth),
            pick(receiver_row, depth),
            pick(receiver_row + channels, depth),
        ],
        axis=0,
    )
    real = jnp.zeros((slots, width), F32)
    imag = jnp.zeros((slots, width), F32)
    for w in range(windows):
        white = lanes_of(LANES + w * width, width)
        rows = jnp.dot(choice, white, preferred_element_type=F32)
        sr, si, rr, ri = [rows[i * slots : (i + 1) * slots] for i in range(4)]
        real += sr * rr + si * ri
        imag += sr * ri - si * rr
    parts = width // LANES
    for i in range(parts):
        lanes = slice(i * LANES, (i + 1) * LANES)
        out[pl.ds(2 * i, slots, stride=2 * parts), :] = real[:, lanes]
        out[pl.ds(2 * i + 1, slots, stride=2 * parts), :] = imag[:, lanes]


def swapped(value, axis, bits):
    peers = lax.axis_size(axis)
    return lax.ppermute(value, axis, [(i, i ^ bits) for i in range(peers)])


def local(traces, offsets, pair_source, pair_recv, pair_hop, pair_owner):
    blocks = lax.axis_size("chan")
    windows = lax.axis_size("win")
    channels = traces.shape[0]
    pair_slots = pair_source.shape[1]
    reach = min(8, (blocks - 1) // 2)
    capacity = 2 * ((pair_slots + blocks - 1) // blocks)
    width = F // windows
    vmem = pl.BlockSpec(memory_space=pltpu.VMEM)
    smem = pl.BlockSpec(memory_space=pltpu.SMEM)
    height = 2 * channels

    table = jnp.asarray(tables())
    pieces = pl.pallas_call(
        whiten_kernel,
        out_shape=[jax.ShapeDtypeStruct((height, width), BF16)] * windows,
        in_specs=[smem] + [pl.BlockSpec(memory_space=pltpu.HBM)] * 3,
        out_specs=[vmem] * windows,
        scratch_shapes=[
            pltpu.VMEM(traces.shape, F32),
            pltpu.SMEM(offsets.shape, jnp.int32),
            pltpu.VMEM(table.shape, F32),
            pltpu.SemaphoreType.DMA((3,)),
            pltpu.VMEM((HIGH * channels, LANES), F32),
            pltpu.VMEM((channels, LANES), F32),
            pltpu.VMEM((GRID_ROWS * channels, LANES), F32),
            pltpu.VMEM((GRID_ROWS * channels, LANES), F32),
            pltpu.VMEM((windows, height, width), BF16),
        ],
        compiler_params=pltpu.CompilerParams(vmem_limit_bytes=LIMIT),
        name="whiten",
    )(lax.axis_index("win").astype(jnp.int32).reshape(1), traces, offsets, table)
    owner = pair_owner.reshape(1, -1)
    spot = jnp.arange(pair_slots)
    same = (pair_owner == owner) & (spot[:, None] < spot[None, :])
    row = owner * capacity + jnp.sum(same.astype(jnp.int32), axis=0, keepdims=True)
    fields = [pair_source, pair_recv, pair_hop, row]
    fields = sum(
        jnp.pad(field, ((i, height - 1 - i), (0, LANES - pair_slots)))
        for i, field in enumerate(fields)
    ).astype(BF16)
    moved = [pieces[0]] + [swapped(pieces[k], "win", k) for k in [*range(2, windows), 1]]
    packed = jnp.concatenate([fields] + moved, axis=1)

    gathered = {0: packed}
    roots = [k + 2 for k in range(4, blocks, 4)]
    for root in roots:
        gathered[root] = swapped(packed, "chan", root)
    for k in range(1, 4):
        gathered[k] = swapped(packed, "chan", k)
    for root in roots:
        for k in range(1, 4):
            gathered[root ^ k] = swapped(gathered[root], "chan", k)
    order = [root ^ k for root in roots for k in (2, 1, 3, 0)] + [3, 2, 1, 0]

    stacked = pl.pallas_call(
        functools.partial(
            stack_kernel, blocks, windows, capacity, reach, pair_slots, width, order
        ),
        out_shape=jax.ShapeDtypeStruct((blocks * capacity * 2 * width // LANES, LANES), F32),
        in_specs=[smem] + [vmem] * blocks,
        out_specs=vmem,
        compiler_params=pltpu.CompilerParams(vmem_limit_bytes=32 << 20),
        name="stack",
    )(lax.axis_index("chan").astype(jnp.int32).reshape(1), *[gathered[k] for k in order])
    stacked = stacked.reshape(blocks * capacity, width // LANES, 2, LANES)
    return stacked.transpose(0, 2, 1, 3).reshape(blocks * capacity, 2, width)


def solution(mesh):
    placed = (
        P("chan", "win"),
        P("win"),
        P("chan", None),
        P("chan", None),
        P("chan", None),
        P("chan", None),
    )
    return jax.shard_map(
        local, mesh=mesh, in_specs=placed, out_specs=P("chan", None, "win"), check_vma=False
    )
```

```python
import functools
import math

import jax
import jax.numpy as jnp
import numpy as np
from jax import lax
from jax.experimental import pallas as pl
from jax.experimental.pallas import tpu as pltpu
from jax.sharding import PartitionSpec as P

NT = 8192
F = 2048
SMOOTH_HALF = 32
LANES = 128
HIGH = NT // LANES
ROWS = F // LANES
GRID_ROWS = 24
F32 = jnp.float32
BF16 = jnp.bfloat16
LIMIT = 55000 << 10


def tables():
    lane = np.arange(LANES)
    high = np.arange(HIGH)
    first = 2 * np.pi / HIGH * (np.outer(np.arange(HIGH) + SMOOTH_HALF, high) % HIGH)
    first = np.concatenate([np.cos(first), -np.sin(first)], axis=0)
    first = np.concatenate([first, first], axis=1)
    twist = 2 * np.pi / NT * (np.outer(high + SMOOTH_HALF, lane) % NT)
    half_row = 2 * (np.arange(GRID_ROWS) - 1)
    half_row = np.concatenate([half_row, half_row + 1])
    second = 2 * np.pi / LANES * (np.outer(half_row, lane) % LANES)
    live = np.tile(np.arange(GRID_ROWS) < ROWS + 2, 2)[:, None]
    cos, sin = np.cos(second) * live, -np.sin(second) * live
    phase = 2 * np.pi / NT * np.arange(NT).reshape(HIGH, LANES)
    rows = [np.cos(phase), np.sin(phase), first, np.cos(twist), -np.sin(twist), cos, sin]
    return np.concatenate(rows, axis=0).astype(np.float32)


def split(value):
    top = value.astype(BF16)
    return top, (value - top.astype(F32)).astype(BF16)


def whiten_kernel(place_ref, traces_far, offsets_far, table_far, *rest):
    outs = rest[:-9]
    traces, offsets, table, arrived, held, means, grid_real, grid_imag, white = rest[-9:]
    copies = [
        pltpu.make_async_copy(offsets_far, offsets, arrived.at[0]),
        pltpu.make_async_copy(traces_far, traces, arrived.at[1]),
        pltpu.make_async_copy(table_far, table, arrived.at[2]),
    ]
    for copy in copies:
        copy.start()
    windows = len(outs)
    channels = traces.shape[0]

    spot = lax.broadcasted_iota(jnp.int32, (3 * LANES, LANES), 0) - LANES
    spot = spot - lax.broadcasted_iota(jnp.int32, (3 * LANES, LANES), 1)
    band = jnp.where(jnp.abs(spot) <= SMOOTH_HALF, 1.0, 0.0).astype(BF16)

    copies[0].wait()
    offset, me = offsets[0], place_ref[0]
    copies[2].wait()
    place = lax.broadcasted_iota(jnp.int32, (1, LANES), 1) == offset % LANES
    turn = offset // LANES
    cos_off = jnp.sum(
        jnp.where(place, table[pl.ds(turn, 1), :], 0.0), axis=1, keepdims=True
    )
    sin_off = jnp.sum(
        jnp.where(place, table[pl.ds(HIGH + turn, 1), :], 0.0), axis=1, keepdims=True
    )
    taper = 0.5 - 0.5 * (table[:HIGH, :] * cos_off + table[HIGH : 2 * HIGH, :] * sin_off)
    at = 2 * HIGH
    first = split(table[at : at + 2 * HIGH, :HIGH])
    first = jnp.concatenate([first[0], first[0], first[1]], axis=1)
    at += 2 * HIGH
    twist_cos = jnp.concatenate([table[at : at + HIGH, :]] * 2, axis=0)
    twist_sin = jnp.concatenate([table[at + HIGH : at + 2 * HIGH, :]] * 2, axis=0)
    at += 2 * HIGH
    cos, sin = table[at : at + 2 * GRID_ROWS, :], table[at + 2 * GRID_ROWS :, :]
    second = split(
        jnp.concatenate(
            [jnp.concatenate([cos, -sin], axis=1), jnp.concatenate([sin, cos], axis=1)], axis=0
        )
    )
    second = jnp.concatenate([second[0], second[0], second[1]], axis=1)

    copies[1].wait()
    lane = lax.broadcasted_iota(jnp.int32, (channels, LANES), 1)
    totals = [jnp.zeros((channels, LANES), F32) for _ in range(4)]
    spare = traces.shape[1] // LANES - HIGH
    for i in range(HIGH):
        piece = traces[:, i * LANES : (i + 1) * LANES]
        if i < spare:
            later = traces[:, (i + HIGH) * LANES : (i + HIGH + 1) * LANES]
            piece = jnp.where(lane + i * LANES >= offset, piece, later)
        held[i * channels : (i + 1) * channels, :] = piece
        totals[i % 4] = totals[i % 4] + piece
    total = (totals[0] + totals[1]) + (totals[2] + totals[3])
    mean = jnp.sum(total, axis=1, keepdims=True) * (1.0 / NT)
    means[...] = jnp.broadcast_to(mean, (channels, LANES))
    inner = []
    for c in range(0, channels, 2):
        segment = [
            (held[pl.ds(c + i, HIGH, stride=channels), :] - means[c + i : c + i + 1, :]) * taper
            for i in range(2)
        ]
        top, low = split(jnp.concatenate(segment, axis=1))
        stacked = jnp.concatenate([top, low, top], axis=0)
        inner.append(jnp.dot(first, stacked, preferred_element_type=F32))
    inner = jnp.concatenate(inner, axis=1)
    lower = lax.broadcasted_iota(jnp.int32, (GRID_ROWS, LANES), 1) < HIGH
    mixed = []
    for c in range(0, channels, 2):
        pair = [slice((c + i) * LANES, (c + i + 1) * LANES) for i in range(2)]
        real = jnp.concatenate([inner[:HIGH, lanes] for lanes in pair], axis=0)
        imag = jnp.concatenate([inner[HIGH:, lanes] for lanes in pair], axis=0)
        top, low = split(
            jnp.concatenate(
                [real * twist_cos - imag * twist_sin, real * twist_sin + imag * twist_cos],
                axis=1,
            )
        )
        mixed.append(jnp.concatenate([top, low, top], axis=1))
    bins_of_all = lax.dot_general(
        second,
        jnp.concatenate(mixed, axis=0),
        (((1,), (1,)), ((), ())),
        preferred_element_type=F32,
    )
    for c in range(0, channels, 2):
        bins = bins_of_all[:, c // 2 * LANES : (c // 2 + 1) * LANES]
        for grid, start in ((grid_real, 0), (grid_imag, 2 * GRID_ROWS)):
            under = bins[start : start + GRID_ROWS]
            over = bins[start + GRID_ROWS : start + 2 * GRID_ROWS]
            rows = jnp.where(lower, under, pltpu.roll(over, HIGH, 1))
            grid[pl.ds(c, GRID_ROWS, stride=channels), :] = rows
            rows = jnp.where(lower, pltpu.roll(under, HIGH, 1), over)
            grid[pl.ds(c + 1, GRID_ROWS, stride=channels), :] = rows

    live = (ROWS + 2) * channels
    real, imag = grid_real[:live, :], grid_imag[:live, :]
    power = (real * real + imag * imag) * (1.0 / (2 * SMOOTH_HALF + 1))
    head = jnp.where(lane >= LANES - SMOOTH_HALF, power[:channels], 0.0)
    tail = jnp.where(lane < SMOOTH_HALF, power[live - channels :], 0.0)
    power = jnp.concatenate([head, power[channels : live - channels], tail], axis=0)
    count = ROWS * channels
    level = jnp.zeros((count, LANES), F32)
    for part in split(power):
        around = [part[i * channels : i * channels + count] for i in range(3)]
        level += jnp.dot(jnp.concatenate(around, axis=1), band, preferred_element_type=F32)
    scale = lax.rsqrt(level + 1e-06)
    kept_real = real[channels : channels + count] * scale
    kept_imag = imag[channels : channels + count] * scale
    part = ROWS // windows
    for i in range(ROWS):
        rows = slice(i * channels, (i + 1) * channels)
        tile = jnp.concatenate([kept_real[rows], kept_imag[rows]], axis=0).astype(BF16)
        white[i // part, :, (i % part) * LANES : (i % part + 1) * LANES] = tile
    for k in range(windows):
        outs[k][...] = white[me ^ k]


def stack_kernel(blocks, windows, capacity, reach, pair_slots, width, order, scalars, *rest):
    pieces, (far_out, out, sent) = rest[:-3], rest[-3:]
    me = scalars[0]
    height = pieces[0].shape[0]
    channels = height // 2
    slots = blocks * capacity

    def lanes_of(start, size):
        return jnp.concatenate(
            [pieces[order.index(b)][:, start : start + size] for b in range(blocks)], axis=0
        )

    meta = lanes_of(0, LANES)

    row = lax.broadcasted_iota(jnp.int32, (slots, LANES), 0)
    lane = lax.broadcasted_iota(jnp.int32, (slots, LANES), 1)
    block = jnp.zeros((slots, LANES), jnp.int32)
    for b in range(1, blocks):
        block = block + (row >= b * capacity).astype(jnp.int32)
    slot = row - block * capacity

    def pick(index, size):
        spot = lax.broadcasted_iota(jnp.int32, (index.shape[0], size), 1)
        if index.shape[1] > 1:
            index = jnp.concatenate([index] * (size // LANES), axis=1)
        return jnp.where(spot == index, 1.0, 0.0)

    base = (block ^ me) * height
    depth = blocks * height
    table = jnp.dot(
        jnp.concatenate([pick(base + i, depth) for i in range(4)], axis=0).astype(BF16),
        meta,
        preferred_element_type=F32,
    )
    source, receiver, hop, target_row = [table[i * slots : (i + 1) * slots] for i in range(4)]
    wanted = (me * capacity + slot).astype(F32)
    chosen = jnp.where((target_row == wanted) & (lane < pair_slots), 1.0, 0.0)

    def value_of(field):
        return jnp.sum(chosen * field, axis=1, keepdims=True).astype(jnp.int32)

    filled = jnp.sum(chosen, axis=1, keepdims=True) > 0.5
    target = block + value_of(hop) - reach
    target = jnp.where(target < 0, target + blocks, target)
    target = jnp.where(target >= blocks, target - blocks, target)
    source_row = base + value_of(source)
    receiver_row = (target ^ me) * height + value_of(receiver)
    source_row = jnp.where(filled, source_row, -depth)
    receiver_row = jnp.where(filled, receiver_row, -depth)
    rows_of = [source_row, source_row + channels, receiver_row, receiver_row + channels]
    parts = width // LANES
    half = slots // 2
    copies = []
    for first in (0, half):
        choice = [pick(index[first : first + half, :1], depth) for index in rows_of]
        choice = jnp.concatenate(choice, axis=0).astype(BF16)
        real = jnp.zeros((half, width), F32)
        imag = jnp.zeros((half, width), F32)
        for w in range(windows):
            white = lanes_of(LANES + w * width, width)
            rows = jnp.dot(choice, white, preferred_element_type=F32)
            sr, si, rr, ri = [rows[i * half : (i + 1) * half] for i in range(4)]
            real += sr * rr + si * ri
            imag += sr * ri - si * rr
        at = 2 * parts * first
        for i in range(parts):
            lanes = slice(i * LANES, (i + 1) * LANES)
            out[pl.ds(at + 2 * i, half, stride=2 * parts), :] = real[:, lanes]
            out[pl.ds(at + 2 * i + 1, half, stride=2 * parts), :] = imag[:, lanes]
        size = 2 * parts * half
        copies.append(
            pltpu.make_async_copy(
                out.at[pl.ds(at, size)], far_out.at[pl.ds(at, size)], sent.at[len(copies)]
            )
        )
        copies[-1].start()
    for copy in copies:
        copy.wait()


def swapped(value, axis, bits):
    peers = lax.axis_size(axis)
    return lax.ppermute(value, axis, [(i, i ^ bits) for i in range(peers)])


def local(traces, offsets, pair_source, pair_recv, pair_hop, pair_owner):
    blocks = lax.axis_size("chan")
    windows = lax.axis_size("win")
    channels = traces.shape[0]
    pair_slots = pair_source.shape[1]
    reach = min(8, (blocks - 1) // 2)
    capacity = 2 * ((pair_slots + blocks - 1) // blocks)
    width = F // windows
    vmem = pl.BlockSpec(memory_space=pltpu.VMEM)
    smem = pl.BlockSpec(memory_space=pltpu.SMEM)
    height = 2 * channels

    table = jnp.asarray(tables())
    pieces = pl.pallas_call(
        whiten_kernel,
        out_shape=[jax.ShapeDtypeStruct((height, width), BF16)] * windows,
        in_specs=[smem] + [pl.BlockSpec(memory_space=pltpu.HBM)] * 3,
        out_specs=[vmem] * windows,
        scratch_shapes=[
            pltpu.VMEM(traces.shape, F32),
            pltpu.SMEM(offsets.shape, jnp.int32),
            pltpu.VMEM(table.shape, F32),
            pltpu.SemaphoreType.DMA((3,)),
            pltpu.VMEM((HIGH * channels, LANES), F32),
            pltpu.VMEM((channels, LANES), F32),
            pltpu.VMEM((GRID_ROWS * channels, LANES), F32),
            pltpu.VMEM((GRID_ROWS * channels, LANES), F32),
            pltpu.VMEM((windows, height, width), BF16),
        ],
        compiler_params=pltpu.CompilerParams(vmem_limit_bytes=LIMIT),
        name="whiten",
    )(lax.axis_index("win").astype(jnp.int32).reshape(1), traces, offsets, table)
    owner = pair_owner.reshape(1, -1)
    spot = jnp.arange(pair_slots)
    same = (pair_owner == owner) & (spot[:, None] < spot[None, :])
    row = owner * capacity + jnp.sum(same.astype(jnp.int32), axis=0, keepdims=True)
    fields = [pair_source, pair_recv, pair_hop, row]
    fields = sum(
        jnp.pad(field, ((i, height - 1 - i), (0, LANES - pair_slots)))
        for i, field in enumerate(fields)
    ).astype(BF16)
    moved = [pieces[0]] + [swapped(pieces[k], "win", k) for k in [*range(2, windows), 1]]
    packed = jnp.concatenate([fields] + moved, axis=1)

    gathered = {0: packed}
    roots = [k + 2 for k in range(4, blocks, 4)]
    for root in roots:
        gathered[root] = swapped(packed, "chan", root)
    for k in range(1, 4):
        gathered[k] = swapped(packed, "chan", k)
    for root in roots:
        for k in range(1, 4):
            gathered[root ^ k] = swapped(gathered[root], "chan", k)
    order = [root ^ k for root in roots for k in (2, 1, 3, 0)] + [3, 2, 1, 0]

    stacked = pl.pallas_call(
        functools.partial(
            stack_kernel, blocks, windows, capacity, reach, pair_slots, width, order
        ),
        out_shape=jax.ShapeDtypeStruct((blocks * capacity * 2 * width // LANES, LANES), F32),
        in_specs=[smem] + [vmem] * blocks,
        out_specs=pl.BlockSpec(memory_space=pltpu.HBM),
        scratch_shapes=[
            pltpu.VMEM((blocks * capacity * 2 * width // LANES, LANES), F32),
            pltpu.SemaphoreType.DMA((2,)),
        ],
        compiler_params=pltpu.CompilerParams(vmem_limit_bytes=32 << 20),
        name="stack",
    )(lax.axis_index("chan").astype(jnp.int32).reshape(1), *[gathered[k] for k in order])
    stacked = stacked.reshape(blocks * capacity, width // LANES, 2, LANES)
    return stacked.transpose(0, 2, 1, 3).reshape(blocks * capacity, 2, width)


def solution(mesh):
    placed = (
        P("chan", "win"),
        P("win"),
        P("chan", None),
        P("chan", None),
        P("chan", None),
        P("chan", None),
    )
    return jax.shard_map(
        local, mesh=mesh, in_specs=placed, out_specs=P("chan", None, "win"), check_vma=False
    )
```

```python
import functools
import math

import jax
import jax.numpy as jnp
import numpy as np
from jax import lax
from jax.experimental import pallas as pl
from jax.experimental.pallas import tpu as pltpu
from jax.sharding import PartitionSpec as P

NT = 8192
F = 2048
SMOOTH_HALF = 32
LANES = 128
HIGH = NT // LANES
ROWS = F // LANES
GRID_ROWS = 24
F32 = jnp.float32
BF16 = jnp.bfloat16
LIMIT = 55000 << 10


def tables():
    lane = np.arange(LANES)
    high = np.arange(HIGH)
    first = 2 * np.pi / HIGH * (np.outer(np.arange(HIGH) + SMOOTH_HALF, high) % HIGH)
    first = np.concatenate([np.cos(first), -np.sin(first)], axis=0)
    first = np.concatenate([first, first], axis=1)
    twist = 2 * np.pi / NT * (np.outer(high + SMOOTH_HALF, lane) % NT)
    half_row = 2 * (np.arange(GRID_ROWS) - 1)
    half_row = np.concatenate([half_row, half_row + 1])
    second = 2 * np.pi / LANES * (np.outer(half_row, lane) % LANES)
    live = np.tile(np.arange(GRID_ROWS) < ROWS + 2, 2)[:, None]
    cos, sin = np.cos(second) * live, -np.sin(second) * live
    phase = 2 * np.pi / NT * np.arange(NT).reshape(HIGH, LANES)
    rows = [np.cos(phase), np.sin(phase), first, np.cos(twist), -np.sin(twist), cos, sin]
    return np.concatenate(rows, axis=0).astype(np.float32)


def split(value):
    top = value.astype(BF16)
    return top, (value - top.astype(F32)).astype(BF16)


def whiten_kernel(place_ref, traces_far, offsets_far, table_far, *rest):
    outs = rest[:-9]
    traces, offsets, table, arrived, held, means, grid_real, grid_imag, white = rest[-9:]
    copies = [
        pltpu.make_async_copy(offsets_far, offsets, arrived.at[0]),
        pltpu.make_async_copy(traces_far, traces, arrived.at[1]),
        pltpu.make_async_copy(table_far, table, arrived.at[2]),
    ]
    for copy in copies:
        copy.start()
    windows = len(outs)
    channels = traces.shape[0]

    spot = lax.broadcasted_iota(jnp.int32, (3 * LANES, LANES), 0) - LANES
    spot = spot - lax.broadcasted_iota(jnp.int32, (3 * LANES, LANES), 1)
    band = jnp.where(jnp.abs(spot) <= SMOOTH_HALF, 1.0, 0.0).astype(BF16)

    copies[0].wait()
    offset, me = offsets[0], place_ref[0]
    copies[2].wait()
    place = lax.broadcasted_iota(jnp.int32, (1, LANES), 1) == offset % LANES
    turn = offset // LANES
    cos_off = jnp.sum(
        jnp.where(place, table[pl.ds(turn, 1), :], 0.0), axis=1, keepdims=True
    )
    sin_off = jnp.sum(
        jnp.where(place, table[pl.ds(HIGH + turn, 1), :], 0.0), axis=1, keepdims=True
    )
    taper = 0.5 - 0.5 * (table[:HIGH, :] * cos_off + table[HIGH : 2 * HIGH, :] * sin_off)
    at = 2 * HIGH
    first = split(table[at : at + 2 * HIGH, :HIGH])
    first = jnp.concatenate([first[0], first[0], first[1]], axis=1)
    at += 2 * HIGH
    twist_cos = jnp.concatenate([table[at : at + HIGH, :]] * 2, axis=0)
    twist_sin = jnp.concatenate([table[at + HIGH : at + 2 * HIGH, :]] * 2, axis=0)
    at += 2 * HIGH
    cos, sin = table[at : at + 2 * GRID_ROWS, :], table[at + 2 * GRID_ROWS :, :]
    second = split(
        jnp.concatenate(
            [jnp.concatenate([cos, -sin], axis=1), jnp.concatenate([sin, cos], axis=1)], axis=0
        )
    )
    second = jnp.concatenate([second[0], second[0], second[1]], axis=1)

    copies[1].wait()
    lane = lax.broadcasted_iota(jnp.int32, (channels, LANES), 1)
    totals = [jnp.zeros((channels, LANES), F32) for _ in range(4)]
    spare = traces.shape[1] // LANES - HIGH
    for i in range(HIGH):
        piece = traces[:, i * LANES : (i + 1) * LANES]
        if i < spare:
            later = traces[:, (i + HIGH) * LANES : (i + HIGH + 1) * LANES]
            piece = jnp.where(lane + i * LANES >= offset, piece, later)
        held[i * channels : (i + 1) * channels, :] = piece
        totals[i % 4] = totals[i % 4] + piece
    total = (totals[0] + totals[1]) + (totals[2] + totals[3])
    mean = jnp.sum(total, axis=1, keepdims=True) * (1.0 / NT)
    means[...] = jnp.broadcast_to(mean, (channels, LANES))
    inner = []
    for c in range(0, channels, 2):
        segment = [
            (held[pl.ds(c + i, HIGH, stride=channels), :] - means[c + i : c + i + 1, :]) * taper
            for i in range(2)
        ]
        top, low = split(jnp.concatenate(segment, axis=1))
        stacked = jnp.concatenate([top, low, top], axis=0)
        inner.append(jnp.dot(first, stacked, preferred_element_type=F32))
    inner = jnp.concatenate(inner, axis=1)
    lower = lax.broadcasted_iota(jnp.int32, (GRID_ROWS, LANES), 1) < HIGH
    mixed = []
    for c in range(0, channels, 2):
        pair = [slice((c + i) * LANES, (c + i + 1) * LANES) for i in range(2)]
        real = jnp.concatenate([inner[:HIGH, lanes] for lanes in pair], axis=0)
        imag = jnp.concatenate([inner[HIGH:, lanes] for lanes in pair], axis=0)
        top, low = split(
            jnp.concatenate(
                [real * twist_cos - imag * twist_sin, real * twist_sin + imag * twist_cos],
                axis=1,
            )
        )
        mixed.append(jnp.concatenate([top, low, top], axis=1))
    bins_of_all = lax.dot_general(
        second,
        jnp.concatenate(mixed, axis=0),
        (((1,), (1,)), ((), ())),
        preferred_element_type=F32,
    )
    for c in range(0, channels, 2):
        bins = bins_of_all[:, c // 2 * LANES : (c // 2 + 1) * LANES]
        for grid, start in ((grid_real, 0), (grid_imag, 2 * GRID_ROWS)):
            under = bins[start : start + GRID_ROWS]
            over = bins[start + GRID_ROWS : start + 2 * GRID_ROWS]
            rows = jnp.where(lower, under, pltpu.roll(over, HIGH, 1))
            grid[pl.ds(c, GRID_ROWS, stride=channels), :] = rows
            rows = jnp.where(lower, pltpu.roll(under, HIGH, 1), over)
            grid[pl.ds(c + 1, GRID_ROWS, stride=channels), :] = rows

    live = (ROWS + 2) * channels
    real, imag = grid_real[:live, :], grid_imag[:live, :]
    power = (real * real + imag * imag) * (1.0 / (2 * SMOOTH_HALF + 1))
    head = jnp.where(lane >= LANES - SMOOTH_HALF, power[:channels], 0.0)
    tail = jnp.where(lane < SMOOTH_HALF, power[live - channels :], 0.0)
    power = jnp.concatenate([head, power[channels : live - channels], tail], axis=0)
    count = ROWS * channels
    around = [
        part[i * channels : i * channels + count] for part in split(power) for i in range(3)
    ]
    level = jnp.dot(
        jnp.concatenate(around, axis=1),
        jnp.concatenate([band, band], axis=0),
        preferred_element_type=F32,
    )
    scale = lax.rsqrt(level + 1e-06)
    kept_real = real[channels : channels + count] * scale
    kept_imag = imag[channels : channels + count] * scale
    part = ROWS // windows
    for i in range(ROWS):
        rows = slice(i * channels, (i + 1) * channels)
        tile = jnp.concatenate([kept_real[rows], kept_imag[rows]], axis=0).astype(BF16)
        white[i // part, :, (i % part) * LANES : (i % part + 1) * LANES] = tile
    for k in range(windows):
        outs[k][...] = white[me ^ k]


def stack_kernel(blocks, windows, capacity, reach, pair_slots, width, order, scalars, *rest):
    pieces, (far_out, out, sent) = rest[:-3], rest[-3:]
    me = scalars[0]
    height = pieces[0].shape[0]
    channels = height // 2
    slots = blocks * capacity

    def lanes_of(start, size):
        return jnp.concatenate(
            [pieces[order.index(b)][:, start : start + size] for b in range(blocks)], axis=0
        )

    meta = lanes_of(0, LANES)

    row = lax.broadcasted_iota(jnp.int32, (slots, LANES), 0)
    lane = lax.broadcasted_iota(jnp.int32, (slots, LANES), 1)
    block = jnp.zeros((slots, LANES), jnp.int32)
    for b in range(1, blocks):
        block = block + (row >= b * capacity).astype(jnp.int32)
    slot = row - block * capacity

    def pick(index, size):
        spot = lax.broadcasted_iota(jnp.int32, (index.shape[0], size), 1)
        if index.shape[1] > 1:
            index = jnp.concatenate([index] * (size // LANES), axis=1)
        return jnp.where(spot == index, 1.0, 0.0)

    base = (block ^ me) * height
    depth = blocks * height
    table = jnp.dot(
        jnp.concatenate([pick(base + i, depth) for i in range(4)], axis=0).astype(BF16),
        meta,
        preferred_element_type=F32,
    )
    source, receiver, hop, target_row = [table[i * slots : (i + 1) * slots] for i in range(4)]
    wanted = (me * capacity + slot).astype(F32)
    chosen = jnp.where((target_row == wanted) & (lane < pair_slots), 1.0, 0.0)

    def value_of(field):
        return jnp.sum(chosen * field, axis=1, keepdims=True).astype(jnp.int32)

    filled = jnp.sum(chosen, axis=1, keepdims=True) > 0.5
    target = block + value_of(hop) - reach
    target = jnp.where(target < 0, target + blocks, target)
    target = jnp.where(target >= blocks, target - blocks, target)
    source_row = base + value_of(source)
    receiver_row = (target ^ me) * height + value_of(receiver)
    source_row = jnp.where(filled, source_row, -depth)
    receiver_row = jnp.where(filled, receiver_row, -depth)
    rows_of = [source_row, source_row + channels, receiver_row, receiver_row + channels]
    parts = width // LANES
    half = slots // 2
    copies = []
    for first in (0, half):
        choice = [pick(index[first : first + half, :1], depth) for index in rows_of]
        choice = jnp.concatenate(choice, axis=0).astype(BF16)
        real = jnp.zeros((half, width), F32)
        imag = jnp.zeros((half, width), F32)
        for w in range(windows):
            white = lanes_of(LANES + w * width, width)
            rows = jnp.dot(choice, white, preferred_element_type=F32)
            sr, si, rr, ri = [rows[i * half : (i + 1) * half] for i in range(4)]
            real += sr * rr + si * ri
            imag += sr * ri - si * rr
        at = 2 * parts * first
        for i in range(parts):
            lanes = slice(i * LANES, (i + 1) * LANES)
            out[pl.ds(at + 2 * i, half, stride=2 * parts), :] = real[:, lanes]
            out[pl.ds(at + 2 * i + 1, half, stride=2 * parts), :] = imag[:, lanes]
        size = 2 * parts * half
        copies.append(
            pltpu.make_async_copy(
                out.at[pl.ds(at, size)], far_out.at[pl.ds(at, size)], sent.at[len(copies)]
            )
        )
        copies[-1].start()
    for copy in copies:
        copy.wait()


def swapped(value, axis, bits):
    peers = lax.axis_size(axis)
    return lax.ppermute(value, axis, [(i, i ^ bits) for i in range(peers)])


def local(traces, offsets, pair_source, pair_recv, pair_hop, pair_owner):
    blocks = lax.axis_size("chan")
    windows = lax.axis_size("win")
    channels = traces.shape[0]
    pair_slots = pair_source.shape[1]
    reach = min(8, (blocks - 1) // 2)
    capacity = 2 * ((pair_slots + blocks - 1) // blocks)
    width = F // windows
    vmem = pl.BlockSpec(memory_space=pltpu.VMEM)
    smem = pl.BlockSpec(memory_space=pltpu.SMEM)
    height = 2 * channels

    table = jnp.asarray(tables())
    pieces = pl.pallas_call(
        whiten_kernel,
        out_shape=[jax.ShapeDtypeStruct((height, width), BF16)] * windows,
        in_specs=[smem] + [pl.BlockSpec(memory_space=pltpu.HBM)] * 3,
        out_specs=[vmem] * windows,
        scratch_shapes=[
            pltpu.VMEM(traces.shape, F32),
            pltpu.SMEM(offsets.shape, jnp.int32),
            pltpu.VMEM(table.shape, F32),
            pltpu.SemaphoreType.DMA((3,)),
            pltpu.VMEM((HIGH * channels, LANES), F32),
            pltpu.VMEM((channels, LANES), F32),
            pltpu.VMEM((GRID_ROWS * channels, LANES), F32),
            pltpu.VMEM((GRID_ROWS * channels, LANES), F32),
            pltpu.VMEM((windows, height, width), BF16),
        ],
        compiler_params=pltpu.CompilerParams(vmem_limit_bytes=LIMIT),
        name="whiten",
    )(lax.axis_index("win").astype(jnp.int32).reshape(1), traces, offsets, table)
    owner = pair_owner.reshape(1, -1)
    spot = jnp.arange(pair_slots)
    same = (pair_owner == owner) & (spot[:, None] < spot[None, :])
    row = owner * capacity + jnp.sum(same.astype(jnp.int32), axis=0, keepdims=True)
    fields = [pair_source, pair_recv, pair_hop, row]
    fields = sum(
        jnp.pad(field, ((i, height - 1 - i), (0, LANES - pair_slots)))
        for i, field in enumerate(fields)
    ).astype(BF16)
    moved = [pieces[0]] + [swapped(pieces[k], "win", k) for k in [*range(2, windows), 1]]
    packed = jnp.concatenate([fields] + moved, axis=1)

    gathered = {0: packed}
    roots = [k + 2 for k in range(4, blocks, 4)]
    for root in roots:
        gathered[root] = swapped(packed, "chan", root)
    for k in range(1, 4):
        gathered[k] = swapped(packed, "chan", k)
    for root in roots:
        for k in range(1, 4):
            gathered[root ^ k] = swapped(gathered[root], "chan", k)
    order = [root ^ k for root in roots for k in (2, 1, 3, 0)] + [3, 2, 1, 0]

    stacked = pl.pallas_call(
        functools.partial(
            stack_kernel, blocks, windows, capacity, reach, pair_slots, width, order
        ),
        out_shape=jax.ShapeDtypeStruct((blocks * capacity * 2 * width // LANES, LANES), F32),
        in_specs=[smem] + [vmem] * blocks,
        out_specs=pl.BlockSpec(memory_space=pltpu.HBM),
        scratch_shapes=[
            pltpu.VMEM((blocks * capacity * 2 * width // LANES, LANES), F32),
            pltpu.SemaphoreType.DMA((2,)),
        ],
        compiler_params=pltpu.CompilerParams(vmem_limit_bytes=32 << 20),
        name="stack",
    )(lax.axis_index("chan").astype(jnp.int32).reshape(1), *[gathered[k] for k in order])
    stacked = stacked.reshape(blocks * capacity, width // LANES, 2, LANES)
    return stacked.transpose(0, 2, 1, 3).reshape(blocks * capacity, 2, width)


def solution(mesh):
    placed = (
        P("chan", "win"),
        P("win"),
        P("chan", None),
        P("chan", None),
        P("chan", None),
        P("chan", None),
    )
    return jax.shard_map(
        local, mesh=mesh, in_specs=placed, out_specs=P("chan", None, "win"), check_vma=False
    )
```

```python
import functools
import math

import jax
import jax.numpy as jnp
import numpy as np
from jax import lax
from jax.experimental import pallas as pl
from jax.experimental.pallas import tpu as pltpu
from jax.sharding import PartitionSpec as P

NT = 8192
F = 2048
SMOOTH_HALF = 32
LANES = 128
HIGH = NT // LANES
ROWS = F // LANES
GRID_ROWS = 24
F32 = jnp.float32
BF16 = jnp.bfloat16
LIMIT = 55000 << 10


def tables():
    lane = np.arange(LANES)
    high = np.arange(HIGH)
    first = 2 * np.pi / HIGH * (np.outer(np.arange(HIGH) + SMOOTH_HALF, high) % HIGH)
    first = np.concatenate([np.cos(first), -np.sin(first)], axis=0)
    first = np.concatenate([first, first], axis=1)
    twist = 2 * np.pi / NT * (np.outer(high + SMOOTH_HALF, lane) % NT)
    half_row = 2 * (np.arange(GRID_ROWS) - 1)
    half_row = np.concatenate([half_row, half_row + 1])
    second = 2 * np.pi / LANES * (np.outer(half_row, lane) % LANES)
    live = np.tile(np.arange(GRID_ROWS) < ROWS + 2, 2)[:, None]
    cos, sin = np.cos(second) * live, -np.sin(second) * live
    phase = 2 * np.pi / NT * np.arange(NT).reshape(HIGH, LANES)
    rows = [np.cos(phase), np.sin(phase), first, np.cos(twist), -np.sin(twist), cos, sin]
    return np.concatenate(rows, axis=0).astype(np.float32)


def split(value):
    top = value.astype(BF16)
    return top, (value - top.astype(F32)).astype(BF16)


def whiten_kernel(place_ref, traces_far, offsets_far, table_far, *rest):
    outs = rest[:-9]
    traces, offsets, table, arrived, held, means, grid_real, grid_imag, white = rest[-9:]
    copies = [
        pltpu.make_async_copy(offsets_far, offsets, arrived.at[0]),
        pltpu.make_async_copy(traces_far, traces, arrived.at[1]),
        pltpu.make_async_copy(table_far, table, arrived.at[2]),
    ]
    for copy in copies:
        copy.start()
    windows = len(outs)
    channels = traces.shape[0]

    spot = lax.broadcasted_iota(jnp.int32, (3 * LANES, LANES), 0) - LANES
    spot = spot - lax.broadcasted_iota(jnp.int32, (3 * LANES, LANES), 1)
    band = jnp.where(jnp.abs(spot) <= SMOOTH_HALF, 1.0, 0.0).astype(BF16)

    copies[0].wait()
    offset, me = offsets[0], place_ref[0]
    copies[2].wait()
    place = lax.broadcasted_iota(jnp.int32, (1, LANES), 1) == offset % LANES
    turn = offset // LANES
    cos_off = jnp.sum(
        jnp.where(place, table[pl.ds(turn, 1), :], 0.0), axis=1, keepdims=True
    )
    sin_off = jnp.sum(
        jnp.where(place, table[pl.ds(HIGH + turn, 1), :], 0.0), axis=1, keepdims=True
    )
    taper = 0.5 - 0.5 * (table[:HIGH, :] * cos_off + table[HIGH : 2 * HIGH, :] * sin_off)
    at = 2 * HIGH
    first = split(table[at : at + 2 * HIGH, :HIGH])
    first = jnp.concatenate([first[0], first[0], first[1]], axis=1)
    at += 2 * HIGH
    twist_cos = jnp.concatenate([table[at : at + HIGH, :]] * 2, axis=0)
    twist_sin = jnp.concatenate([table[at + HIGH : at + 2 * HIGH, :]] * 2, axis=0)
    at += 2 * HIGH
    cos, sin = table[at : at + 2 * GRID_ROWS, :], table[at + 2 * GRID_ROWS :, :]
    second = split(
        jnp.concatenate(
            [jnp.concatenate([cos, -sin], axis=1), jnp.concatenate([sin, cos], axis=1)], axis=0
        )
    )
    second = jnp.concatenate([second[0], second[0], second[1]], axis=1)

    copies[1].wait()
    lane = lax.broadcasted_iota(jnp.int32, (channels, LANES), 1)
    totals = [jnp.zeros((channels, LANES), F32) for _ in range(4)]
    spare = traces.shape[1] // LANES - HIGH
    for i in range(HIGH):
        piece = traces[:, i * LANES : (i + 1) * LANES]
        if i < spare:
            later = traces[:, (i + HIGH) * LANES : (i + HIGH + 1) * LANES]
            piece = jnp.where(lane + i * LANES >= offset, piece, later)
        held[i * channels : (i + 1) * channels, :] = piece
        totals[i % 4] = totals[i % 4] + piece
    total = (totals[0] + totals[1]) + (totals[2] + totals[3])
    mean = jnp.sum(total, axis=1, keepdims=True) * (1.0 / NT)
    means[...] = jnp.broadcast_to(mean, (channels, LANES))
    inner = []
    for c in range(0, channels, 2):
        segment = [
            (held[pl.ds(c + i, HIGH, stride=channels), :] - means[c + i : c + i + 1, :]) * taper
            for i in range(2)
        ]
        top, low = split(jnp.concatenate(segment, axis=1))
        stacked = jnp.concatenate([top, low, top], axis=0)
        inner.append(jnp.dot(first, stacked, preferred_element_type=F32))
    inner = jnp.concatenate(inner, axis=1)
    lower = lax.broadcasted_iota(jnp.int32, (GRID_ROWS, LANES), 1) < HIGH
    mixed = []
    for c in range(0, channels, 2):
        pair = [slice((c + i) * LANES, (c + i + 1) * LANES) for i in range(2)]
        real = jnp.concatenate([inner[:HIGH, lanes] for lanes in pair], axis=0)
        imag = jnp.concatenate([inner[HIGH:, lanes] for lanes in pair], axis=0)
        top, low = split(
            jnp.concatenate(
                [real * twist_cos - imag * twist_sin, real * twist_sin + imag * twist_cos],
                axis=1,
            )
        )
        mixed.append(jnp.concatenate([top, low, top], axis=1))
    bins_of_all = lax.dot_general(
        second,
        jnp.concatenate(mixed, axis=0),
        (((1,), (1,)), ((), ())),
        preferred_element_type=F32,
    )
    for c in range(0, channels, 2):
        bins = bins_of_all[:, c // 2 * LANES : (c // 2 + 1) * LANES]
        for grid, start in ((grid_real, 0), (grid_imag, 2 * GRID_ROWS)):
            under = bins[start : start + GRID_ROWS]
            over = bins[start + GRID_ROWS : start + 2 * GRID_ROWS]
            rows = jnp.where(lower, under, pltpu.roll(over, HIGH, 1))
            grid[pl.ds(c, GRID_ROWS, stride=channels), :] = rows
            rows = jnp.where(lower, pltpu.roll(under, HIGH, 1), over)
            grid[pl.ds(c + 1, GRID_ROWS, stride=channels), :] = rows

    live = (ROWS + 2) * channels
    real, imag = grid_real[:live, :], grid_imag[:live, :]
    power = (real * real + imag * imag) * (1.0 / (2 * SMOOTH_HALF + 1))
    head = jnp.where(lane >= LANES - SMOOTH_HALF, power[:channels], 0.0)
    tail = jnp.where(lane < SMOOTH_HALF, power[live - channels :], 0.0)
    power = jnp.concatenate([head, power[channels : live - channels], tail], axis=0)
    count = ROWS * channels
    around = [
        part[i * channels : i * channels + count] for part in split(power) for i in range(3)
    ]
    level = jnp.dot(
        jnp.concatenate(around, axis=1),
        jnp.concatenate([band, band], axis=0),
        preferred_element_type=F32,
    )
    scale = lax.rsqrt(level + 1e-06)
    kept_real = real[channels : channels + count] * scale
    kept_imag = imag[channels : channels + count] * scale
    part = ROWS // windows
    for i in range(ROWS):
        rows = slice(i * channels, (i + 1) * channels)
        tile = jnp.concatenate([kept_real[rows], kept_imag[rows]], axis=0).astype(BF16)
        white[i // part, :, (i % part) * LANES : (i % part + 1) * LANES] = tile
    for k in range(windows):
        outs[k][...] = white[me ^ k]


def stack_kernel(blocks, windows, capacity, reach, pair_slots, width, order, scalars, *rest):
    pieces, (far_out, out, sent) = rest[:-3], rest[-3:]
    me = scalars[0]
    height = pieces[0].shape[0]
    channels = height // 2
    slots = blocks * capacity

    def lanes_of(start, size):
        return jnp.concatenate(
            [pieces[order.index(b)][:, start : start + size] for b in range(blocks)], axis=0
        )

    meta = lanes_of(0, LANES)

    row = lax.broadcasted_iota(jnp.int32, (slots, LANES), 0)
    lane = lax.broadcasted_iota(jnp.int32, (slots, LANES), 1)
    block = jnp.zeros((slots, LANES), jnp.int32)
    for b in range(1, blocks):
        block = block + (row >= b * capacity).astype(jnp.int32)
    slot = row - block * capacity

    def pick(index, size):
        spot = lax.broadcasted_iota(jnp.int32, (index.shape[0], size), 1)
        if index.shape[1] > 1:
            index = jnp.concatenate([index] * (size // LANES), axis=1)
        return jnp.where(spot == index, 1.0, 0.0)

    base = (block ^ me) * height
    depth = blocks * height
    table = jnp.dot(
        jnp.concatenate([pick(base + i, depth) for i in range(4)], axis=0).astype(BF16),
        meta,
        preferred_element_type=F32,
    )
    source, receiver, hop, target_row = [table[i * slots : (i + 1) * slots] for i in range(4)]
    wanted = (me * capacity + slot).astype(F32)
    chosen = jnp.where((target_row == wanted) & (lane < pair_slots), 1.0, 0.0)

    def value_of(field):
        return jnp.sum(chosen * field, axis=1, keepdims=True).astype(jnp.int32)

    filled = jnp.sum(chosen, axis=1, keepdims=True) > 0.5
    target = block + value_of(hop) - reach
    target = jnp.where(target < 0, target + blocks, target)
    target = jnp.where(target >= blocks, target - blocks, target)
    source_row = base + value_of(source)
    receiver_row = (target ^ me) * height + value_of(receiver)
    source_row = jnp.where(filled, source_row, -depth)
    receiver_row = jnp.where(filled, receiver_row, -depth)
    rows_of = [source_row, source_row + channels, receiver_row, receiver_row + channels]
    parts = width // LANES
    cut = slots - 16
    copies = []
    for first, half in ((0, cut), (cut, slots - cut)):
        choice = [pick(index[first : first + half, :1], depth) for index in rows_of]
        choice = jnp.concatenate(choice, axis=0).astype(BF16)
        real = jnp.zeros((half, width), F32)
        imag = jnp.zeros((half, width), F32)
        for w in range(windows):
            white = lanes_of(LANES + w * width, width)
            rows = jnp.dot(choice, white, preferred_element_type=F32)
            sr, si, rr, ri = [rows[i * half : (i + 1) * half] for i in range(4)]
            real += sr * rr + si * ri
            imag += sr * ri - si * rr
        at = 2 * parts * first
        for i in range(parts):
            lanes = slice(i * LANES, (i + 1) * LANES)
            out[pl.ds(at + 2 * i, half, stride=2 * parts), :] = real[:, lanes]
            out[pl.ds(at + 2 * i + 1, half, stride=2 * parts), :] = imag[:, lanes]
        size = 2 * parts * half
        copies.append(
            pltpu.make_async_copy(
                out.at[pl.ds(at, size)], far_out.at[pl.ds(at, size)], sent.at[len(copies)]
            )
        )
        copies[-1].start()
    for copy in copies:
        copy.wait()


def swapped(value, axis, bits):
    peers = lax.axis_size(axis)
    return lax.ppermute(value, axis, [(i, i ^ bits) for i in range(peers)])


def local(traces, offsets, pair_source, pair_recv, pair_hop, pair_owner):
    blocks = lax.axis_size("chan")
    windows = lax.axis_size("win")
    channels = traces.shape[0]
    pair_slots = pair_source.shape[1]
    reach = min(8, (blocks - 1) // 2)
    capacity = 2 * ((pair_slots + blocks - 1) // blocks)
    width = F // windows
    vmem = pl.BlockSpec(memory_space=pltpu.VMEM)
    smem = pl.BlockSpec(memory_space=pltpu.SMEM)
    height = 2 * channels

    table = jnp.asarray(tables())
    pieces = pl.pallas_call(
        whiten_kernel,
        out_shape=[jax.ShapeDtypeStruct((height, width), BF16)] * windows,
        in_specs=[smem] + [pl.BlockSpec(memory_space=pltpu.HBM)] * 3,
        out_specs=[vmem] * windows,
        scratch_shapes=[
            pltpu.VMEM(traces.shape, F32),
            pltpu.SMEM(offsets.shape, jnp.int32),
            pltpu.VMEM(table.shape, F32),
            pltpu.SemaphoreType.DMA((3,)),
            pltpu.VMEM((HIGH * channels, LANES), F32),
            pltpu.VMEM((channels, LANES), F32),
            pltpu.VMEM((GRID_ROWS * channels, LANES), F32),
            pltpu.VMEM((GRID_ROWS * channels, LANES), F32),
            pltpu.VMEM((windows, height, width), BF16),
        ],
        compiler_params=pltpu.CompilerParams(vmem_limit_bytes=LIMIT),
        name="whiten",
    )(lax.axis_index("win").astype(jnp.int32).reshape(1), traces, offsets, table)
    owner = pair_owner.reshape(1, -1)
    spot = jnp.arange(pair_slots)
    same = (pair_owner == owner) & (spot[:, None] < spot[None, :])
    row = owner * capacity + jnp.sum(same.astype(jnp.int32), axis=0, keepdims=True)
    fields = [pair_source, pair_recv, pair_hop, row]
    fields = sum(
        jnp.pad(field, ((i, height - 1 - i), (0, LANES - pair_slots)))
        for i, field in enumerate(fields)
    ).astype(BF16)
    moved = [pieces[0]] + [swapped(pieces[k], "win", k) for k in [*range(2, windows), 1]]
    packed = jnp.concatenate([fields] + moved, axis=1)

    gathered = {0: packed}
    roots = [k + 2 for k in range(4, blocks, 4)]
    for root in roots:
        gathered[root] = swapped(packed, "chan", root)
    for k in range(1, 4):
        gathered[k] = swapped(packed, "chan", k)
    for root in roots:
        for k in range(1, 4):
            gathered[root ^ k] = swapped(gathered[root], "chan", k)
    order = [root ^ k for root in roots for k in (2, 1, 3, 0)] + [3, 2, 1, 0]

    stacked = pl.pallas_call(
        functools.partial(
            stack_kernel, blocks, windows, capacity, reach, pair_slots, width, order
        ),
        out_shape=jax.ShapeDtypeStruct((blocks * capacity * 2 * width // LANES, LANES), F32),
        in_specs=[smem] + [vmem] * blocks,
        out_specs=pl.BlockSpec(memory_space=pltpu.HBM),
        scratch_shapes=[
            pltpu.VMEM((blocks * capacity * 2 * width // LANES, LANES), F32),
            pltpu.SemaphoreType.DMA((2,)),
        ],
        compiler_params=pltpu.CompilerParams(vmem_limit_bytes=32 << 20),
        name="stack",
    )(lax.axis_index("chan").astype(jnp.int32).reshape(1), *[gathered[k] for k in order])
    stacked = stacked.reshape(blocks * capacity, width // LANES, 2, LANES)
    return stacked.transpose(0, 2, 1, 3).reshape(blocks * capacity, 2, width)


def solution(mesh):
    placed = (
        P("chan", "win"),
        P("win"),
        P("chan", None),
        P("chan", None),
        P("chan", None),
        P("chan", None),
    )
    return jax.shard_map(
        local, mesh=mesh, in_specs=placed, out_specs=P("chan", None, "win"), check_vma=False
    )
```
